128 devices in a mesh: expert: 8 (over y_hi, x), tensor: 16 (over z, y_lo, core).
Axes of the slice: x: 4, y: 4 (y_hi: 2, y_lo: 2; y = y_hi * 2 + y_lo), z: 4, core: 2. Of those that a mesh axis runs over, the one named last changes fastest.
Arguments:
- hidden_in: bfloat16 [16384, 3584], P(('expert', 'tensor')), may hold values from -50 to 50
- norm_gain: float32 [3584], replicated, may hold values from 0.1 to 1.9
- upstream: bfloat16 [16384, 3584], P(('expert', 'tensor')), may hold values from -20 to 20
- routes: int32 [16384, 4], P(('expert', 'tensor')), may hold values from 0 to 127, all different within a row; in each aligned block of 128 rows (0 to 127, 128 to 255, ...) at most 6 rows name the same one
- combine_fixed: int32 [16384, 4], P(('expert', 'tensor')), may hold values from 6554 to 65535
- w_gate: bfloat16 [128, 3584, 1024], P(('expert', 'tensor')), may hold values from -0.09375 to 0.09375
- w_up: bfloat16 [128, 3584, 1024], P(('expert', 'tensor')), may hold values from -0.09375 to 0.09375
- w_down: bfloat16 [128, 1024, 3584], P(('expert', 'tensor')), may hold values from -0.1875 to 0.1875
Outputs:
- input_grad: bfloat16 [16384, 3584], P(('expert', 'tensor'))
- gain_grad: float32 [3584], replicated
- combine_grad: bfloat16 [16384, 4], P(('expert', 'tensor'))
The draws below stay inside these ranges and needn't reach their ends.
Inputs may be any that keep to these rules, and one draw needn't show every extreme that they name: `routes`: each row names 4 different experts. Among the 128 rows of one device no expert is named by more than 6 rows, and in every draw some expert is named by exactly 6 rows of some device.
All inputs are finite; a program needn't handle non-finite values.
Results may differ from the reference program's by a relative error of at most 0.0071.
Values may be sent and summed in bfloat16 or wider, within the bound.
A program may use at most 128 MiB of HBM per device.

```python
import math
import jax
import jax.numpy as jnp
import numpy as np
from jax import lax

D = 3584
H = 1024
TOPK = 4
TOK_DEV = 128
EXPERTS = 128
TOKENS = 16384
CAP = 6


def draw_hidden_in(key, part):
    key = jax.random.fold_in(key, 11)
    row_key, value_key = jax.random.split(key)
    values = jnp.clip(jax.random.normal(value_key, (TOKENS, D), jnp.float32), -5.0, 5.0)
    row_scale = jnp.exp(jax.random.uniform(row_key, (TOKENS, 1), jnp.float32, 0.0, math.log(10.0)))
    return (values * row_scale).astype(jnp.bfloat16)


def draw_upstream(key, part):
    key = jax.random.fold_in(key, 23)
    value_key = jax.random.fold_in(key, 1)
    rising = 1.0 + 2.0 * jnp.arange(TOKENS, dtype=jnp.float32)[:, None] / TOKENS
    values = jnp.clip(jax.random.normal(value_key, (TOKENS, D), jnp.float32), -5.0, 5.0)
    return (values * rising).astype(jnp.bfloat16)


def set_ends(array, rng, smallest, high):
    extent = array.shape
    index_at = [jax.random.randint(jax.random.fold_in(rng, axis), (), 0, extent[axis]) for axis in range(len(extent))]
    array = array.at[tuple(index_at)].set(smallest)
    longest = extent.index(max(extent))
    index_at[longest] = (index_at[longest] + 1) % extent[longest]
    return array.at[tuple(index_at)].set(high)


def levels(own_key, shape, cuts, smallest, top_value):
    level, own = 1.0, jax.random.fold_in(own_key, 6)
    for axis_at, parts in cuts:
        heights = jnp.exp(jax.random.uniform(jax.random.fold_in(own, axis_at), (parts,), jnp.float32, smallest / len(cuts), top_value / len(cuts)))
        level = level * jnp.repeat(heights, shape[axis_at] // parts).reshape([-1 if axis == axis_at else 1 for axis in range(len(shape))])
    return level


def assign_block(key, own, number, rows, count, top, most, lean):
    order = jax.random.permutation(key, count)
    crowded, usual = load_shares(count, rows * top, most, lean, True), load_shares(count, rows * top, most, lean, False)
    places = jnp.arange(count)

    def named(tallies, offset_by):
        used = int((tallies > 0).sum())
        fixed = max(1, used // 4)
        moved = fixed + (places - fixed + offset_by * (used - fixed)) % max(1, count - fixed)
        return jnp.zeros((count,), jnp.int32).at[order[jnp.where(places < fixed, places, moved)]].set(jnp.asarray(tallies, jnp.int32))

    tallies = jnp.where(number % 4 == 0, named(crowded, number // 4), named(usual, number - number // 4 - 1))
    mixed = jax.random.permutation(jax.random.fold_in(own, 3), count)
    source_of, receiver = mixed[0:count // 2 * 2:2], mixed[1:count // 2 * 2:2]
    room = jnp.minimum(tallies[source_of] - 1, most - tallies[receiver]) // 2
    room = jnp.where((source_of == order[0]) | (receiver == order[0]) | (tallies[receiver] == 0), 0, jnp.maximum(room, 0))
    moved = jax.random.randint(jax.random.fold_in(own, 4), (count // 2,), 0, 1 << 20) % (room + 1)
    tallies = tallies.at[source_of].add(-moved).at[receiver].add(moved)
    items = jnp.searchsorted(jnp.cumsum(tallies), jnp.arange(rows * top), side="right").astype(jnp.int32)
    table = items.reshape(top, rows).T
    table = table[jax.random.permutation(jax.random.fold_in(own, 1), rows)]
    offset_by = jax.random.randint(jax.random.fold_in(own, 2), (rows, 1), 0, top)
    return jnp.take_along_axis(table, (jnp.arange(top)[None, :] + offset_by) % top, axis=1)


def load_shares(number_of, total, limit, lean, full):
    loads = [(1 << 20) // math.isqrt(standing ** lean) + 1 for standing in range(1, number_of + 1)]
    largest = limit if full else min(limit, max(-(-total // number_of), total * loads[0] // sum(loads)))
    least = 1 if total - largest >= number_of - 1 else 0
    holding, spare = [largest] + [least] * (number_of - 1), total - largest - least * (number_of - 1)
    while spare > 0:
        free = [i for i in range(1, number_of) if holding[i] < largest] or [i for i in range(1, number_of) if holding[i] < limit]
        pool, budget = sum([loads[i] for i in free]), spare
        for i in free:
            addition = min(limit - holding[i], max(1, budget * loads[i] // pool), spare)
            holding[i] = holding[i] + addition
            spare = spare - addition
    return np.array(holding)


def normal_values(own_key, shape, width, bound, pieces=(), kind=jnp.bfloat16):
    array = width * jax.random.normal(own_key, shape, jnp.float32)
    if pieces:
        array = array * levels(own_key, shape, pieces, -0.22, 0.18)
    return jnp.clip(array, -bound, bound).astype(kind)


def setup_inputs(seed: int = 0) -> dict:
    splits = jax.random.split(jax.random.key(seed), 9)
    hidden_in = draw_hidden_in(jax.random.fold_in(splits[8], 71), 0)
    norm_gain = jnp.clip(1.0 + 0.18 * jax.random.normal(splits[1], (D,), jnp.float32), 0.1, 1.9)
    upstream = draw_upstream(jax.random.fold_in(splits[8], 71), 0)
    routes_keys = jax.random.split(jax.random.fold_in(splits[3], 1), TOKENS // TOK_DEV)
    routes_turns = jax.random.permutation(jax.random.fold_in(splits[3], 3), TOKENS // TOK_DEV)
    routes = jax.vmap(lambda own, number: assign_block(jax.random.fold_in(splits[3], 2), own, number, TOK_DEV, EXPERTS, TOPK, CAP, 2))(routes_keys, routes_turns).reshape((TOKENS, TOPK))
    combine_fixed = set_ends(jax.random.randint(splits[4], (TOKENS, TOPK), 6554, 65536), jax.random.fold_in(splits[4], 1), 6554, 65535).astype(jnp.int32)
    w_gate = normal_values(splits[5], (EXPERTS, D, H), D ** -0.5, 0.09375, ((0, 128),))
    w_up = normal_values(splits[6], (EXPERTS, D, H), D ** -0.5, 0.09375, ((0, 128),))
    w_down = normal_values(splits[7], (EXPERTS, H, D), H ** -0.5, 0.1875, ((0, 128),))
    return dict(hidden_in=hidden_in, norm_gain=norm_gain, upstream=upstream, routes=routes, combine_fixed=combine_fixed, w_gate=w_gate, w_up=w_up, w_down=w_down)


CONTRACT = (((1,), (1,)), ((), ()))

def recompute(rows_in, weight_gate, weight_up):
    gate_pre = jnp.dot(rows_in, weight_gate, preferred_element_type=jnp.float32)
    up_pre = jnp.dot(rows_in, weight_up, preferred_element_type=jnp.float32)
    return (gate_pre, up_pre)

def finish(gate_pre, up_pre, grads_in, scale_in, weight_gate, weight_up, weight_down):
    back_proj = lax.dot_general(grads_in, weight_down, CONTRACT, preferred_element_type=jnp.float32)
    gate_sig = jax.nn.sigmoid(gate_pre)
    gate_act = gate_pre * gate_sig
    comb_grad = lax.optimization_barrier(jnp.sum(gate_act * up_pre * back_proj, axis=1)).astype(jnp.bfloat16)
    scaled = scale_in.astype(jnp.float32)[:, None] * back_proj
    d_gate = (scaled * up_pre * gate_sig * (1.0 + gate_pre * (1.0 - gate_sig))).astype(jnp.bfloat16)
    d_up = (scaled * gate_act).astype(jnp.bfloat16)
    slot_grad = lax.dot_general(d_gate, weight_gate, CONTRACT, preferred_element_type=jnp.float32)
    slot_grad = slot_grad + lax.dot_general(d_up, weight_up, CONTRACT, preferred_element_type=jnp.float32)
    return (slot_grad.astype(jnp.bfloat16), comb_grad)

def reference(hidden_in, norm_gain, upstream, routes, combine_fixed, w_gate, w_up, w_down):
    tokens_all = hidden_in.shape[0]
    blocks = tokens_all // TOK_DEV
    hidden_f = hidden_in.astype(jnp.float32)
    inv_rms = lax.rsqrt(lax.optimization_barrier(jnp.mean(hidden_f * hidden_f, axis=1, keepdims=True)) + 1e-06)
    unit_rows = hidden_f * inv_rms
    normed = (unit_rows * norm_gain[None, :]).astype(jnp.bfloat16)
    weight = (combine_fixed.astype(jnp.float32) / 65536.0).astype(jnp.bfloat16)
    flat_routes = routes.reshape(blocks, TOK_DEV * TOPK).astype(jnp.int32)
    expert_ids = jnp.arange(EXPERTS, dtype=jnp.int32)
    onehot = (flat_routes[:, :, None] == expert_ids[None, None, :]).astype(jnp.int32)
    position = lax.optimization_barrier(jnp.sum((jnp.cumsum(onehot, axis=1) - 1) * onehot, axis=2)).astype(jnp.int32)
    block_ids = jnp.arange(blocks, dtype=jnp.int32)[:, None]
    slot_index = ((block_ids * EXPERTS + flat_routes) * CAP + position).reshape(-1).astype(jnp.int32)
    slot_table = jnp.full((blocks * EXPERTS * CAP,), -1, jnp.int32)
    slot_table = slot_table.at[slot_index].set(jnp.arange(tokens_all * TOPK, dtype=jnp.int32))
    slot_table = slot_table.reshape(blocks, EXPERTS, CAP)
    weight_flat = weight.reshape(-1)

    def expert_step(state_pair, expert_index):
        normed_grad, comb_flat = state_pair
        pair_ids = lax.dynamic_index_in_dim(slot_table, expert_index, 1, keepdims=False).reshape(-1)
        is_live = pair_ids >= 0
        safe_ids = jnp.where(is_live, pair_ids, 0).astype(jnp.int32)
        token_ids = (safe_ids // TOPK).astype(jnp.int32)
        rows_in = jnp.where(is_live[:, None], normed[token_ids], 0)
        grads_in = jnp.where(is_live[:, None], upstream[token_ids], 0)
        scale_in = jnp.where(is_live, weight_flat[safe_ids], 0)
        weight_gate = lax.dynamic_index_in_dim(w_gate, expert_index, 0, keepdims=False)
        weight_up = lax.dynamic_index_in_dim(w_up, expert_index, 0, keepdims=False)
        weight_down = lax.dynamic_index_in_dim(w_down, expert_index, 0, keepdims=False)
        gate_pre, up_pre = recompute(rows_in, weight_gate, weight_up)
        slot_grad, comb_grad = finish(gate_pre, up_pre, grads_in, scale_in, weight_gate, weight_up, weight_down)
        normed_grad = normed_grad.at[token_ids].add(jnp.where(is_live[:, None], slot_grad.astype(jnp.float32), 0.0))
        comb_flat = comb_flat.at[safe_ids].add(jnp.where(is_live, comb_grad.astype(jnp.float32), 0.0))
        return ((normed_grad, comb_flat), None)
    start_state = (jnp.zeros((tokens_all, D), jnp.float32), jnp.zeros((tokens_all * TOPK,), jnp.float32))
    final_state, unused = lax.scan(expert_step, start_state, jnp.arange(EXPERTS, dtype=jnp.int32))
    normed_grad, comb_flat = final_state
    combine_grad = comb_flat.reshape(tokens_all, TOPK).astype(jnp.bfloat16)
    gain_grad = lax.optimization_barrier(jnp.sum(normed_grad * unit_rows, axis=0))
    scaled_grad = normed_grad * norm_gain[None, :]
    project = lax.optimization_barrier(jnp.mean(scaled_grad * unit_rows, axis=1, keepdims=True))
    input_grad = (inv_rms * (scaled_grad - unit_rows * project)).astype(jnp.bfloat16)
    return (input_grad, gain_grad, combine_grad)
```

```python
import jax
import jax.numpy as jnp
from jax import lax
from jax.experimental import pallas as pl
from jax.experimental.pallas import tpu as pltpu
from jax.sharding import PartitionSpec as P

MESH = pl.DeviceIdType.MESH
BF = jnp.bfloat16
F32 = jnp.float32
D = 3584
H = 1024
TOK = 128
CW = 512
NC = D // CW
ROWS = 768
MSG = 48
GTOK = 1024
NT = (((1,), (1,)), ((), ()))
PLANE = ((1, 0), (0, 1), (3, 0), (0, 3), (2, 0), (0, 2), (1, 1), (3, 3), (1, 3), (3, 1), (2, 1), (1, 2), (3, 2), (2, 3), (2, 2))
NS = 3


def device(x, y, z, c):
    return {"expert": (y // 2) * 4 + x, "tensor": z * 4 + (y % 2) * 2 + c}


def mm(a, b):
    return jnp.dot(a, b, preferred_element_type=F32)


def mm_nt(a, b):
    return lax.dot_general(a, b, NT, preferred_element_type=F32)


def kernel(
    hid_ref, gain_ref, ups_ref, rts_ref, cmb_ref, wg_ref, wu_ref, wd_ref,
    out_ref, gout_ref, cout_ref,
    tok, tokaux, gat, gatt, sbuf, saux, rcv, raux, acc_g, acc_u, acc_b,
    wdb, wgb, wub, caux, cret, pbuf, paux, qbuf, qaux, sibaux, ringaux, inv_s, proj_s,
    gall, gring, gsib, gstage,
    w_sem, ag_ss, ag_rr, ag_sr, a_ss, a_rs, a_self, x_ss, x_rs, x_self,
    r_rs, r_self, p_ss, p_rs, q_ss, q_rs, g_ss, g_rs, free_sib, free_ring,
):
    e_i, t_i = lax.axis_index("expert"), lax.axis_index("tensor")
    x, y, z, c = e_i % 4, (e_i // 4) * 2 + (t_i // 2) % 2, t_i // 4, t_i % 2
    me = e_i * 16 + t_i
    plane_me = y * 4 + x
    src_me = c * 4 + z
    sib = device(x, y, z, 1 - c)
    ring = [device(x, y, (z + d) % 4, c) for d in (1, 2, 3)]
    plane = [
        (((y + dy) % 4) * 4 + (x + dx) % 4, device((x + dx) % 4, (y + dy) % 4, z, c)) for dx, dy in PLANE
    ]

    def rows(at, size, align=16):
        return pl.ds(pl.multiple_of(at, align), size)

    def put(src, dst, ss, rs, to):
        pltpu.make_async_remote_copy(
            src_ref=src, dst_ref=dst, send_sem=ss, recv_sem=rs, device_id=to, device_id_type=MESH
        ).start()

    def await_bytes(ref, sem):
        pltpu.make_async_copy(ref, ref, sem).wait()

    def wd_copy(n):
        return pltpu.make_async_copy(
            wd_ref.at[0, :, pl.ds(pl.multiple_of(n * CW, CW), CW)], wdb.at[n % 2], w_sem.at[0, n % 2]
        )

    def wgu_copies(n):
        at = rows(jnp.where(n >= NC, n - NC, n) * CW, CW, CW)
        return (
            pltpu.make_async_copy(wg_ref.at[0, at], wgb.at[n % 2], w_sem.at[1, n % 2]),
            pltpu.make_async_copy(wu_ref.at[0, at], wub.at[n % 2], w_sem.at[2, n % 2]),
        )

    for n in (0, 1):
        wd_copy(n).start()
        for cp in wgu_copies(n):
            cp.start()

    bar = pltpu.get_barrier_semaphore()
    everyone = [sib] + ring + [d for _, d in plane]
    for d in everyone:
        pl.semaphore_signal(bar, inc=1, device_id=d, device_id_type=MESH)

    lane = lax.broadcasted_iota(jnp.int32, (TOK, 128), 1)
    dense = jnp.zeros((TOK, 128), F32)
    for k in range(4):
        wk = cmb_ref[:, k : k + 1].astype(F32) * (1.0 / 65536.0)
        dense = jnp.where(rts_ref[:, k : k + 1] == lane, wk, dense)
    own = rows(src_me * TOK, TOK, TOK)
    tokaux[own, :] = dense.astype(BF)
    for k in range(NC):
        tok[k, own, :] = ups_ref[:, k * CW : (k + 1) * CW]

    pl.semaphore_wait(bar, len(everyone))

    def ag_send(k):
        for d in [*ring, sib]:
            rs = ag_sr.at[k] if d is sib else ag_rr.at[k]
            put(tok.at[k, own], tok.at[k, own], ag_ss.at[k], rs, d)

    def ag_forward(k):
        await_bytes(tok.at[k, pl.ds(0, 3 * TOK)], ag_rr.at[k])
        for d in (1, 2, 3):
            at = rows((c * 4 + (z + d) % 4) * TOK, TOK, TOK)
            put(tok.at[k, at], tok.at[k, at], ag_ss.at[k], ag_sr.at[k], sib)

    def ag_await(k):
        await_bytes(tok.at[k, pl.ds(0, 4 * TOK)], ag_sr.at[k])
        await_bytes(tok.at[k, pl.ds(0, 7 * TOK)], ag_ss.at[k])

    for d in [*ring, sib]:
        put(tokaux.at[own], tokaux.at[own], x_ss.at[0], x_rs.at[1 if d is sib else 0], d)
    ag_send(0)
    ag_send(1)

    total = jnp.zeros((TOK, CW), F32)
    for k in range(NC):
        h = hid_ref[:, k * CW : (k + 1) * CW].astype(F32)
        total = total + h * h
    inv = lax.rsqrt(jnp.sum(total, axis=1, keepdims=True) * (1.0 / D) + 1e-06)
    inv_s[...] = jnp.broadcast_to(inv, (TOK, 128))
    for k in range(NC):
        cols = slice(k * CW, (k + 1) * CW)
        unit = hid_ref[:, cols].astype(F32) * inv
        tok[NC + k, own, :] = (unit * gain_ref[:, cols]).astype(BF)

    await_bytes(tokaux.at[pl.ds(0, 3 * TOK)], x_rs.at[0])
    for d in (1, 2, 3):
        at = rows((c * 4 + (z + d) % 4) * TOK, TOK, TOK)
        put(tokaux.at[at], tokaux.at[at], x_ss.at[0], x_rs.at[1], sib)
    await_bytes(tokaux.at[pl.ds(0, 4 * TOK)], x_rs.at[1])
    await_bytes(tokaux.at[pl.ds(0, 7 * TOK)], x_ss.at[0])

    slot = lax.broadcasted_iota(jnp.int32, (8, ROWS), 1)
    peer = jnp.zeros((8, ROWS), jnp.int32)
    for m in range(1, 16):
        peer = peer + (slot >= MSG * m).astype(jnp.int32)
    rest = slot - MSG * peer
    source = jnp.zeros((8, ROWS), jnp.int32)
    for m in range(1, 8):
        source = source + (rest >= 6 * m).astype(jnp.int32)
    place = (rest - 6 * source + 1).astype(F32)
    py = lax.shift_right_logical(peer, 2)
    px = lax.bitwise_and(peer, 3)
    peer_expert = (
        (lax.shift_right_logical(py, 1) * 4 + px) * 16 + z * 4 + lax.bitwise_and(py, 1) * 2 + c
    )
    pick = (
        lax.broadcasted_iota(jnp.int32, (128, ROWS), 0) == jnp.broadcast_to(peer_expert[0:1], (128, ROWS))
    ).astype(F32).astype(BF)
    below = (
        lax.broadcasted_iota(jnp.int32, (TOK, TOK), 0) > lax.broadcasted_iota(jnp.int32, (TOK, TOK), 1)
    ).astype(F32).astype(BF)
    for s in range(8):
        named = (tokaux[s * TOK : (s + 1) * TOK, :].astype(F32) != 0.0).astype(F32)
        code = (mm(below, named.astype(BF)) + 1.0) * named
        want = jnp.where(source[0:1] == s, place[0:1], -1.0)
        hot = (mm(code.astype(BF), pick) == jnp.broadcast_to(want, (TOK, ROWS))).astype(F32)
        gatt[s * TOK : (s + 1) * TOK, :] = hot.astype(BF)
        gat[:, s * TOK : (s + 1) * TOK] = jnp.transpose(hot).astype(BF)

    saux[...] = mm(gat[...], tokaux[...]).astype(BF)
    mine = rows(plane_me * MSG, MSG)
    for p, d in plane:
        put(saux.at[rows(p * MSG, MSG)], raux.at[mine], x_ss.at[1], x_rs.at[2], d)
    pltpu.make_async_copy(saux.at[mine], raux.at[mine], x_self.at[0]).start()

    def spread(buf, dst, rs, self_sem):
        for p, d in plane:
            put(sbuf.at[buf, rows(p * MSG, MSG)], dst.at[mine], a_ss.at[buf], rs, d)
        pltpu.make_async_copy(sbuf.at[buf, mine], dst.at[mine], self_sem).start()

    def await_spread(dst, rs, self_sem):
        await_bytes(dst.at[pl.ds(0, 15 * MSG)], rs)
        await_bytes(dst.at[pl.ds(0, MSG)], self_sem)

    def await_sbuf(buf):
        await_bytes(sbuf.at[buf, pl.ds(0, 15 * MSG)], a_ss.at[buf])

    ag_forward(0)
    RB = 256

    def dispatch(i, carry):
        @pl.when(i < 2 * NC)
        def _():
            buf = lax.rem(i, NS)
            ag_await(i)

            @pl.when(i >= NS)
            def _():
                await_sbuf(buf)

            def gather(r, cc):
                at = rows(r * RB, RB, RB)
                sbuf[buf, at, :] = mm(gat[at, :], tok[i]).astype(BF)
                return cc

            lax.fori_loop(0, ROWS // RB, gather, 0)
            spread(buf, rcv.at[i], a_rs.at[i], a_self.at[i])

        @pl.when(i + 2 < 2 * NC)
        def _():
            ag_send(i + 2)

        @pl.when(i + 1 < 2 * NC)
        def _():
            ag_forward(i + 1)

        @pl.when(i >= 2)
        def _():
            j = i - 2
            await_spread(rcv.at[j], a_rs.at[j], a_self.at[j])

            @pl.when(j < NC)
            def _():
                wd_copy(j).wait()

                def step(r, cc):
                    at = rows(r * RB, RB, RB)
                    got = mm_nt(rcv[j, at, :], wdb[lax.rem(j, 2)])

                    @pl.when(j == 0)
                    def _():
                        acc_b[at, :] = got

                    @pl.when(j > 0)
                    def _():
                        acc_b[at, :] += got

                    return cc

                lax.fori_loop(0, ROWS // RB, step, 0)

                @pl.when(j + 2 < NC)
                def _():
                    wd_copy(j + 2).start()

            @pl.when(j >= NC)
            def _():
                n = j - NC
                for cp in wgu_copies(n):
                    cp.wait()

                def step(r, cc):
                    at = rows(r * RB, RB, RB)
                    for acc, w in ((acc_g, wgb), (acc_u, wub)):
                        got = mm(rcv[j, at, :], w[lax.rem(n, 2)])

                        @pl.when(n == 0)
                        def _():
                            acc[at, :] = got

                        @pl.when(n > 0)
                        def _():
                            acc[at, :] += got

                    return cc

                lax.fori_loop(0, ROWS // RB, step, 0)
                for cp in wgu_copies(n + 2):
                    cp.start()

        return carry

    lax.fori_loop(0, 2 * NC + 2, dispatch, 0)

    pl.semaphore_signal(free_sib, inc=1, device_id=sib, device_id_type=MESH)
    for d in ring:
        pl.semaphore_signal(free_ring, inc=1, device_id=d, device_id_type=MESH)

    await_bytes(raux.at[pl.ds(0, 15 * MSG)], x_rs.at[2])
    await_bytes(raux.at[pl.ds(0, MSG)], x_self.at[0])
    await_bytes(saux.at[pl.ds(0, 15 * MSG)], x_ss.at[1])
    AB = 64
    alane = lax.broadcasted_iota(jnp.int32, (AB, 128), 1)

    def activate(r, cc):
        at = rows(r * AB, AB, AB)
        scale = jnp.sum(jnp.where(alane == me, raux[at, :].astype(F32), 0.0), axis=1, keepdims=True)
        comb = jnp.zeros((AB, 1), F32)
        for half in range(2):
            cols = slice(half * CW, (half + 1) * CW)
            gate, up, back = acc_g[at, cols], acc_u[at, cols], acc_b[at, cols]
            sig = jax.nn.sigmoid(gate)
            act = gate * sig
            comb = comb + jnp.sum(act * up * back, axis=1, keepdims=True)
            scaled = scale * back
            rcv[half, at, :] = (scaled * up * sig * (1.0 + gate * (1.0 - sig))).astype(BF)
            rcv[2 + half, at, :] = (scaled * act).astype(BF)
        caux[at, :] = jnp.where(alane == me, comb, 0.0).astype(BF)
        return cc

    lax.fori_loop(0, ROWS // AB, activate, 0)

    for p, d in plane:
        put(caux.at[rows(p * MSG, MSG)], cret.at[mine], x_ss.at[2], x_rs.at[3], d)
    pltpu.make_async_copy(caux.at[mine], cret.at[mine], x_self.at[1]).start()

    half_me, half_sib = rows(c * 512, 512, 512), rows((1 - c) * 512, 512, 512)

    def own_part(k):
        return pl.ds(0, 512), pl.ds(pl.multiple_of(lax.rem(k, 2) * CW, CW), CW)

    def grad_part(k):
        return rows(lax.div(k, 2) * TOK, TOK, TOK), pl.ds(pl.multiple_of(lax.rem(k, 2) * CW, CW), CW)

    def send_back(i):
        n = i + NC
        buf = lax.rem(i + 2 * NC, NS)
        await_sbuf(buf)
        for cp in wgu_copies(n):
            cp.wait()

        def step(r, gsum):
            at = rows(r * RB, RB, RB)
            got = mm_nt(rcv[0, at, :], wgb[lax.rem(n, 2), :, 0:CW])
            got = got + mm_nt(rcv[1, at, :], wgb[lax.rem(n, 2), :, CW:H])
            got = got + mm_nt(rcv[2, at, :], wub[lax.rem(n, 2), :, 0:CW])
            got = got + mm_nt(rcv[3, at, :], wub[lax.rem(n, 2), :, CW:H])
            cut = got.astype(BF)
            sbuf[buf, at, :] = cut
            prod = cut.astype(F32) * rcv[NC + i, at, :].astype(F32)
            return gsum + jnp.sum(prod, axis=0, keepdims=True)

        gsum = lax.fori_loop(0, ROWS // RB, step, jnp.zeros((1, CW), F32))
        gstage[:, pl.ds(pl.multiple_of(i * CW, CW), CW)] = gsum
        spread(buf, tok.at[i], r_rs.at[i], r_self.at[i])

        @pl.when(i + 2 < NC)
        def _():
            for cp in wgu_copies(n + 2):
                cp.start()

    def combine(k):
        b = lax.rem(k, 2)
        await_spread(tok.at[k], r_rs.at[k], r_self.at[k])

        @pl.when(k >= 2)
        def _():
            await_bytes(pbuf.at[b], p_ss.at[b])

        ret = tok.at[k]
        pbuf[b] = mm(gatt[half_sib, :], ret[0:ROWS, :]).astype(BF)
        put(pbuf.at[b], tok.at[NC + k, pl.ds(0, 512)], p_ss.at[b], p_rs.at[k], sib)
        at, cols = own_part(k)
        acc_g[at, cols] = mm(gatt[half_me, :], ret[0:ROWS, :])

    def scatter(k):
        b = lax.rem(k, 2)
        await_bytes(tok.at[NC + k, pl.ds(0, 512)], p_rs.at[k])

        @pl.when(k >= 2)
        def _():
            await_bytes(qbuf.at[b], q_ss.at[b])

        _, cols = own_part(k)
        for d in (1, 2, 3):
            at = rows(((z + d) % 4) * TOK, TOK, TOK)
            qbuf[b, (d - 1) * TOK : d * TOK, :] = (acc_g[at, cols] + tok[NC + k, at, :].astype(F32)).astype(BF)
            put(
                qbuf.at[b, pl.ds((d - 1) * TOK, TOK)], tok.at[NC + k, pl.ds(512 + (d - 1) * TOK, TOK)],
                q_ss.at[b], q_rs.at[k], ring[d - 1],
            )
        at = rows(z * TOK, TOK, TOK)
        grow, gcol = grad_part(k)
        acc_u[grow, gcol] = acc_g[at, cols] + tok[NC + k, at, :].astype(F32)

    def settle(k):
        await_bytes(tok.at[NC + k, pl.ds(512, 384)], q_rs.at[k])
        grow, gcol = grad_part(k)
        grad = acc_u[grow, gcol]
        for d in range(3):
            grad = grad + tok[NC + k, 512 + d * TOK : 512 + (d + 1) * TOK, :].astype(F32)
        cols = pl.ds(pl.multiple_of(k * CW, CW), CW)
        scaled = grad * gain_ref[:, cols]
        acc_u[grow, gcol] = scaled
        proj_s[...] += scaled * (hid_ref[:, cols].astype(F32) * inv_s[:, 0:1])

    proj_s[...] = jnp.zeros_like(proj_s)

    def back(i, carry):
        @pl.when(i < NC)
        def _():
            send_back(i)

        @pl.when(i == 2)
        def _():
            pl.semaphore_wait(free_sib, 1)
            pl.semaphore_wait(free_ring, 3)

        @pl.when(i == 3)
        def _():
            await_bytes(cret.at[pl.ds(0, 15 * MSG)], x_rs.at[3])
            await_bytes(cret.at[pl.ds(0, MSG)], x_self.at[1])
            await_bytes(caux.at[pl.ds(0, 15 * MSG)], x_ss.at[2])
            paux[...] = mm(gatt[half_sib, :], cret[...]).astype(BF)
            put(paux, sibaux, x_ss.at[3], x_rs.at[4], sib)

        @pl.when(i == 5)
        def _():
            await_bytes(sibaux, x_rs.at[4])
            await_bytes(paux, x_ss.at[3])
            qaux[...] = (mm(gatt[half_me, :], cret[...]) + sibaux[...].astype(F32)).astype(BF)
            for d in (1, 2, 3):
                at = rows(((z + d) % 4) * TOK, TOK, TOK)
                put(qaux.at[at], ringaux.at[pl.ds((d - 1) * TOK, TOK)], x_ss.at[4], x_rs.at[5], ring[d - 1])

        @pl.when(i == NC - 1)
        def _():
            gall[plane_me] = gstage[...]
            for _, d in plane:
                put(gall.at[plane_me], gall.at[plane_me], g_ss.at[0], g_rs.at[0], d)

        @pl.when(jnp.logical_and(i >= 2, i < NC + 2))
        def _():
            combine(i - 2)

        @pl.when(jnp.logical_and(i >= 3, i < NC + 3))
        def _():
            scatter(i - 3)

        @pl.when(i == NC)
        def _():
            await_bytes(gall.at[pl.ds(0, 15)], g_rs.at[0])
            await_bytes(gall.at[pl.ds(0, 15)], g_ss.at[0])
            gring[z] = jnp.sum(gall[...], axis=0)
            for d in ring:
                put(gring.at[z], gring.at[z], g_ss.at[1], g_rs.at[1], d)

        @pl.when(i == NC + 1)
        def _():
            await_bytes(gring.at[pl.ds(0, 3)], g_rs.at[1])
            await_bytes(gring.at[pl.ds(0, 3)], g_ss.at[1])
            gsib[c] = gring[0] + gring[1] + gring[2] + gring[3]
            put(gsib.at[c], gsib.at[c], g_ss.at[2], g_rs.at[2], sib)

        @pl.when(i >= 4)
        def _():
            settle(i - 4)

        return carry

    lax.fori_loop(0, NC + 4, back, 0)

    project = jnp.sum(proj_s[...], axis=1, keepdims=True) * (1.0 / D)
    inv = inv_s[:, 0:1]
    for k in range(NC):
        cols = slice(k * CW, (k + 1) * CW)
        scaled = acc_u[(k // 2) * TOK : (k // 2 + 1) * TOK, (k % 2) * CW : (k % 2 + 1) * CW]
        unit = hid_ref[:, cols].astype(F32) * inv
        out_ref[:, cols] = (inv * (scaled - unit * project)).astype(BF)

    await_bytes(gsib.at[pl.ds(0, 1)], g_rs.at[2])
    await_bytes(gsib.at[pl.ds(0, 1)], g_ss.at[2])
    gout_ref[...] = (gsib[0] + gsib[1]) / gain_ref[...]

    await_bytes(ringaux, x_rs.at[5])
    await_bytes(ringaux, x_ss.at[4])
    mine_q = rows(z * TOK, TOK, TOK)
    cfin = qaux[mine_q, :].astype(F32)
    for d in range(3):
        cfin = cfin + ringaux[d * TOK : (d + 1) * TOK, :].astype(F32)
    for k in range(4):
        got = jnp.sum(jnp.where(rts_ref[:, k : k + 1] == lane, cfin, 0.0), axis=1, keepdims=True)
        cout_ref[:, k : k + 1] = got.astype(BF)

    for b in range(NS):
        await_sbuf(b)
    for b in range(2):
        await_bytes(pbuf.at[b], p_ss.at[b])
        await_bytes(qbuf.at[b], q_ss.at[b])


def shards(hidden_in, norm_gain, upstream, routes, combine_fixed, w_gate, w_up, w_down):
    vm = pl.BlockSpec(memory_space=pltpu.VMEM)
    hbm = pl.BlockSpec(memory_space=pl.ANY)
    dma = pltpu.SemaphoreType.DMA
    out, gain_grad, combine_grad = pl.pallas_call(
        kernel,
        out_shape=(
            jax.ShapeDtypeStruct((TOK, D), BF),
            jax.ShapeDtypeStruct((1, D), F32),
            jax.ShapeDtypeStruct((TOK, 4), BF),
        ),
        in_specs=[vm, vm, vm, vm, vm, hbm, hbm, hbm],
        out_specs=(vm, vm, vm),
        scratch_shapes=[
            pltpu.VMEM((2 * NC, GTOK, CW), BF),
            pltpu.VMEM((GTOK, 128), BF),
            pltpu.VMEM((ROWS, GTOK), BF),
            pltpu.VMEM((GTOK, ROWS), BF),
            pltpu.VMEM((NS, ROWS, CW), BF),
            pltpu.VMEM((ROWS, 128), BF),
            pltpu.VMEM((2 * NC, ROWS, CW), BF),
            pltpu.VMEM((ROWS, 128), BF),
            pltpu.VMEM((ROWS, H), F32),
            pltpu.VMEM((ROWS, H), F32),
            pltpu.VMEM((ROWS, H), F32),
            pltpu.VMEM((2, H, CW), BF),
            pltpu.VMEM((2, CW, H), BF),
            pltpu.VMEM((2, CW, H), BF),
            pltpu.VMEM((ROWS, 128), BF),
            pltpu.VMEM((ROWS, 128), BF),
            pltpu.VMEM((2, 512, CW), BF),
            pltpu.VMEM((512, 128), BF),
            pltpu.VMEM((2, 384, CW), BF),
            pltpu.VMEM((512, 128), BF),
            pltpu.VMEM((512, 128), BF),
            pltpu.VMEM((384, 128), BF),
            pltpu.VMEM((TOK, 128), F32),
            pltpu.VMEM((TOK, CW), F32),
            pltpu.VMEM((16, 1, D), F32),
            pltpu.VMEM((4, 1, D), F32),
            pltpu.VMEM((2, 1, D), F32),
            pltpu.VMEM((1, D), F32),
            dma((3, 2)),
            dma((2 * NC,)),
            dma((2 * NC,)),
            dma((2 * NC,)),
            dma((NS,)),
            dma((2 * NC,)),
            dma((2 * NC,)),
            dma((5,)),
            dma((6,)),
            dma((2,)),
            dma((NC,)),
            dma((NC,)),
            dma((2,)),
            dma((NC,)),
            dma((2,)),
            dma((NC,)),
            dma((3,)),
            dma((3,)),
            pltpu.SemaphoreType.REGULAR,
            pltpu.SemaphoreType.REGULAR,
        ],
        compiler_params=pltpu.CompilerParams(
            collective_id=0, has_side_effects=True, vmem_limit_bytes=62 * 2**20
        ),
        cost_estimate=pl.CostEstimate(flops=50 * 10**9, bytes_accessed=40 * 10**6, transcendentals=10**6),
    )(hidden_in, norm_gain[None, :], upstream, routes, combine_fixed, w_gate, w_up, w_down)
    return out, gain_grad.reshape(D), combine_grad


def solution(mesh):
    split = ("expert", "tensor")
    in_specs = (
        P(split, None),
        P(),
        P(split, None),
        P(split, None),
        P(split, None),
        P(split, None, None),
        P(split, None, None),
        P(split, None, None),
    )
    out_specs = (P(split, None), P(), P(split, None))
    return jax.shard_map(shards, mesh=mesh, in_specs=in_specs, out_specs=out_specs, check_vma=False)
```

```python
import jax
import jax.numpy as jnp
from jax import lax
from jax.experimental import pallas as pl
from jax.experimental.pallas import tpu as pltpu
from jax.sharding import PartitionSpec as P

MESH = pl.DeviceIdType.MESH
BF = jnp.bfloat16
F32 = jnp.float32
D = 3584
H = 1024
TOK = 128
CW = 512
NC = D // CW
ROWS = 768
MSG = 48
GTOK = 1024
HALF = TOK // 2
NT = (((1,), (1,)), ((), ()))
PLANE = ((1, 0), (0, 1), (3, 0), (0, 3), (2, 0), (0, 2), (1, 1), (3, 3), (1, 3), (3, 1), (2, 1), (1, 2), (3, 2), (2, 3), (2, 2))
NS = 4
RB = 256
AB = 64
L1, L2, L3 = 7, 5, 3
K1, K2, K3, K4 = 2, 4, 5, 7
LAG = 3


def device(x, y, z, c):
    return {"expert": (y // 2) * 4 + x, "tensor": z * 4 + (y % 2) * 2 + c}


def mm(a, b):
    return jnp.dot(a, b, preferred_element_type=F32)


def mm_nt(a, b):
    return lax.dot_general(a, b, NT, preferred_element_type=F32)


def rows(at, size, align=16):
    return pl.ds(pl.multiple_of(at, align), size)


class Frame:
    def __init__(self, a, x, y, z, c):
        self.is0 = (a - 1) * (a - 2) // 2
        self.is1 = a * (2 - a)
        self.is2 = a * (a - 1) // 2
        self.u = (1 - self.is1) * y + self.is1 * z
        self.v = (1 - self.is0) * x + self.is0 * z
        self.r = self.is2 * z + self.is0 * x + self.is1 * y
        self.c = c

    def coords(self, u, v, r):
        return (
            self.is0 * r + (1 - self.is0) * v,
            self.is1 * r + (1 - self.is1) * u,
            self.is2 * r + self.is0 * v + self.is1 * u,
        )

    def ring(self, d):
        return device(*self.coords(self.u, self.v, (self.r + d) % 4), self.c)

    def peers(self):
        for dv, du in PLANE:
            u, v = (self.u + du) % 4, (self.v + dv) % 4
            yield u * 4 + v, device(*self.coords(u, v, self.r), self.c)

    def place(self):
        return self.u * 4 + self.v


def kernel(
    hid_ref, gain_ref, ups_ref, rts_ref, cmb_ref, wg_ref, wu_ref, wd_ref,
    out_ref, gout_ref, cout_ref,
    tok, tokaux, gat, gatt, perm, sbuf, saux, rcv, raux, canon, acc, hid, gain, turn,
    wdb, wgb, wub, caux, cret, pbuf, paux, q1buf, q2buf, qaux, sibaux, ringaux, inv_s, proj_s,
    gall, gring, gsib, gstage,
    i_sem, w_sem, ag_ss, ag_r1, ag_r2, ag_sr, aux_r, aux_s, aux_ss, a_ss, a_rs, a_self, x_ss, x_rs, x_self,
    r_rs, r_self, p_ss, p_rs, q1_ss, q1_rs, q2_ss, q2_rs, g_ss, g_rs, free_sib, free_ring,
):
    e_i, t_i = lax.axis_index("expert"), lax.axis_index("tensor")
    x, y, z, c = e_i % 4, (e_i // 4) * 2 + (t_i // 2) % 2, t_i // 4, t_i % 2
    me = e_i * 16 + t_i
    sib = device(x, y, z, 1 - c)

    def frame(a):
        return Frame(a, x, y, z, c)

    def axis(i):
        return lax.rem(i + 1, 3)

    def back_axis(k):
        return lax.rem(k + 2, 3)

    def own(f):
        return rows((c * 4 + f.r) * TOK, TOK, TOK)

    def ring_rows(f, d):
        return rows((c * 4 + (f.r + d) % 4) * TOK, TOK, TOK)

    def put(src, dst, ss, rs, to):
        pltpu.make_async_remote_copy(
            src_ref=src, dst_ref=dst, send_sem=ss, recv_sem=rs, device_id=to, device_id_type=MESH
        ).start()

    def await_bytes(ref, sem):
        pltpu.make_async_copy(ref, ref, sem).wait()

    def await_once(ref, sem, n):
        await_bytes(ref.at[pl.ds(0, n)], sem)

    zf = frame(2)
    bar = pltpu.get_barrier_semaphore()
    everyone = [sib]
    for dx in range(4):
        for dy in range(4):
            for dz in range(4):
                if 0 in (dx, dy, dz) and (dx or dy or dz):
                    everyone.append(device((x + dx) % 4, (y + dy) % 4, (z + dz) % 4, c))
    for d in everyone:
        pl.semaphore_signal(bar, inc=1, device_id=d, device_id_type=MESH)

    for k in range(NC):
        pltpu.make_async_copy(
            ups_ref.at[:, pl.ds(k * CW, CW)], tok.at[k, own(frame((k + 1) % 3))], i_sem.at[0]
        ).start()
    pltpu.make_async_copy(hid_ref, hid, i_sem.at[1]).start()

    def wd_copy(n):
        return pltpu.make_async_copy(
            wd_ref.at[0, :, pl.ds(pl.multiple_of(n * CW, CW), CW)], wdb.at[n % 2], w_sem.at[0, n % 2]
        )

    def wgu_copies(n):
        at = rows(jnp.where(n >= NC, n - NC, n) * CW, CW, CW)
        return (
            pltpu.make_async_copy(wg_ref.at[0, at], wgb.at[n % 2], w_sem.at[1, n % 2]),
            pltpu.make_async_copy(wu_ref.at[0, at], wub.at[n % 2], w_sem.at[2, n % 2]),
        )

    for n in (0, 1):
        wd_copy(n).start()
        for cp in wgu_copies(n):
            cp.start()

    lane = lax.broadcasted_iota(jnp.int32, (TOK, 128), 1)
    turn[0:4, :] = rts_ref[...].astype(F32)
    turn[4:8, :] = cmb_ref[...].astype(F32) * (1.0 / 65536.0)
    turned = jnp.transpose(turn[...])
    lane_f = lane.astype(F32)
    dense = jnp.zeros((TOK, 128), F32)
    for k in range(4):
        dense = jnp.where(turned[:, k : k + 1] == lane_f, turned[:, 4 + k : 5 + k], dense)
    dense = dense.astype(BF)
    for a in range(3):
        tokaux[a, own(frame(a)), :] = dense
    for r in range(D // 128):
        gain[:, r * 128 : (r + 1) * 128] = gain_ref[r : r + 1, :]

    pl.semaphore_wait(bar, len(everyone))

    for a in (1, 2, 0):
        f = frame(a)
        at = own(f)
        for d in (1, 3, 2):
            put(tokaux.at[a, at], tokaux.at[a, at], aux_ss.at[a], aux_r.at[a], f.ring(d))
        put(tokaux.at[a, at], tokaux.at[a, at], aux_ss.at[a], aux_s.at[a], sib)

    def ag_first(i):
        f = frame(axis(i))
        at = own(f)
        put(tok.at[i, at], tok.at[i, at], ag_ss.at[i], ag_r1.at[i], f.ring(1))
        put(tok.at[i, at], tok.at[i, at], ag_ss.at[i], ag_r1.at[i], f.ring(3))
        put(tok.at[i, at], tok.at[i, at], ag_ss.at[i], ag_sr.at[i], sib)

    def ag_second(i):
        f = frame(axis(i))
        await_once(tok.at[i], ag_r1.at[i], 2 * TOK)
        for d, part in ((3, 0), (1, HALF)):
            at = rows((c * 4 + (f.r + d) % 4) * TOK + part, HALF, HALF)
            put(tok.at[i, at], tok.at[i, at], ag_ss.at[i], ag_r2.at[i], f.ring(4 - d))
        for d in (3, 1):
            at = ring_rows(f, d)
            put(tok.at[i, at], tok.at[i, at], ag_ss.at[i], ag_sr.at[i], sib)

    def ag_third(i):
        f = frame(axis(i))
        await_once(tok.at[i], ag_r2.at[i], TOK)
        at = ring_rows(f, 2)
        put(tok.at[i, at], tok.at[i, at], ag_ss.at[i], ag_sr.at[i], sib)

    await_once(tok.at[0], i_sem.at[0], 7 * TOK)
    for i in range(3):
        ag_first(i)

    slot = lax.broadcasted_iota(jnp.int32, (8, ROWS), 1)
    peer = jnp.zeros((8, ROWS), jnp.int32)
    for m in range(1, 16):
        peer = peer + (slot >= MSG * m).astype(jnp.int32)
    rest = slot - MSG * peer
    source = jnp.zeros((8, ROWS), jnp.int32)
    for m in range(1, 8):
        source = source + (rest >= 6 * m).astype(jnp.int32)
    place = rest - 6 * source
    pu, pv = lax.shift_right_logical(peer, 2), lax.bitwise_and(peer, 3)
    sc, sr = lax.shift_right_logical(source, 2), lax.bitwise_and(source, 3)

    def build(a):
        f = frame(a)
        await_once(tokaux.at[a], aux_s.at[a], 4 * TOK)
        await_once(tokaux.at[a], aux_ss.at[a], 7 * TOK)
        px, py, pz = f.coords(pu, pv, jnp.zeros_like(pu) + f.r)
        expert = (
            (lax.shift_right_logical(py, 1) * 4 + px) * 16 + pz * 4 + lax.bitwise_and(py, 1) * 2 + c
        )
        pick = (
            lax.broadcasted_iota(jnp.int32, (128, ROWS), 0) == jnp.broadcast_to(expert[0:1], (128, ROWS))
        ).astype(F32).astype(BF)
        below = (
            lax.broadcasted_iota(jnp.int32, (TOK, TOK), 0) > lax.broadcasted_iota(jnp.int32, (TOK, TOK), 1)
        ).astype(F32).astype(BF)
        for s in range(8):
            part = slice(s * TOK, (s + 1) * TOK)
            named = (tokaux[a, part, :].astype(F32) != 0.0).astype(F32)
            code = (mm(below, named.astype(BF)) + 1.0) * named
            want = jnp.where(source[0:1] == s, (place[0:1] + 1).astype(F32), -1.0)
            hot = (mm(code.astype(BF), pick) == jnp.broadcast_to(want, (TOK, ROWS))).astype(F32)
            gatt[a, part, :] = hot.astype(BF)
            gat[a, :, part] = jnp.transpose(hot).astype(BF)

    def swaps():
        swap_x = (pu * 4 + sr) * MSG + (sc * 4 + pv) * 6 + place
        swap_y = (sr * 4 + pv) * MSG + (sc * 4 + pu) * 6 + place
        at = lax.broadcasted_iota(jnp.int32, (ROWS, ROWS), 0)
        for a, to in ((0, swap_x), (1, swap_y)):
            perm[a] = (at == jnp.broadcast_to(to[0:1], (ROWS, ROWS))).astype(F32).astype(BF)

    def norm():
        await_bytes(hid, i_sem.at[1])
        total = jnp.zeros((TOK, CW), F32)
        for k in range(NC):
            h = hid[:, k * CW : (k + 1) * CW].astype(F32)
            total = total + h * h
        inv = lax.rsqrt(jnp.sum(total, axis=1, keepdims=True) * (1.0 / D) + 1e-06)
        inv_s[...] = jnp.broadcast_to(inv, (TOK, 128))
        for k in range(NC):
            cols = slice(k * CW, (k + 1) * CW)
            unit = hid[:, cols].astype(F32) * inv
            tok[NC + k, own(frame((NC + k + 1) % 3)), :] = (unit * gain[:, cols]).astype(BF)

    norm()
    for a in (1, 2, 0):
        f = frame(a)
        await_once(tokaux.at[a], aux_r.at[a], 3 * TOK)
        for d in (1, 3, 2):
            at = ring_rows(f, d)
            put(tokaux.at[a, at], tokaux.at[a, at], aux_ss.at[a], aux_s.at[a], sib)
    for i in range(3):
        ag_second(i)
    for i in range(3, 6):
        ag_first(i)
    build(1)
    for i in range(3):
        ag_third(i)
    swaps()
    ag_second(3)

    def spread(f, buf, dst, rs, self_sem):
        mine = rows(f.place() * MSG, MSG)
        for p, d in f.peers():
            put(sbuf.at[buf, rows(p * MSG, MSG)], dst.at[mine], a_ss.at[buf], rs, d)
        pltpu.make_async_copy(sbuf.at[buf, mine], dst.at[mine], self_sem).start()

    def await_spread(dst, rs, self_sem):
        await_once(dst, rs, 15 * MSG)
        await_once(dst, self_sem, MSG)

    def await_sbuf(buf):
        await_once(sbuf.at[buf], a_ss.at[buf], 15 * MSG)

    def by_rows(step):
        def body(r, cc):
            step(rows(r * RB, RB, RB))
            return cc

        lax.fori_loop(0, ROWS // RB, body, 0)

    def reorder(a, src, dst):
        @pl.when(a == 2)
        def _():
            dst[...] = src[...]

        @pl.when(a != 2)
        def _():
            def step(at):
                dst[at, :] = mm(perm[jnp.minimum(a, 1), at, :], src[...]).astype(BF)

            by_rows(step)

    def dispatch(i, carry):
        @pl.when(i < 2 * NC)
        def _():
            buf = lax.rem(i, NS)
            a = axis(i)

            @pl.when(jnp.logical_and(i >= 1, i < 3))
            def _():
                build(a)

            await_once(tok.at[i], ag_sr.at[i], 4 * TOK)

            @pl.when(i >= NS)
            def _():
                await_sbuf(buf)

            def gather(at):
                sbuf[buf, at, :] = mm(gat[a, at, :], tok[i]).astype(BF)

            by_rows(gather)
            await_once(tok.at[i], ag_ss.at[i], 7 * TOK)
            spread(frame(a), buf, rcv.at[i], a_rs.at[i], a_self.at[i])

        @pl.when(i == 1)
        def _():
            saux[...] = mm(gat[2], tokaux[2]).astype(BF)
            mine = rows(zf.place() * MSG, MSG)
            for p, d in zf.peers():
                put(saux.at[rows(p * MSG, MSG)], raux.at[mine], x_ss.at[1], x_rs.at[2], d)
            pltpu.make_async_copy(saux.at[mine], raux.at[mine], x_self.at[0]).start()

        @pl.when(i >= LAG)
        def _():
            j = i - LAG
            await_spread(rcv.at[j], a_rs.at[j], a_self.at[j])

            @pl.when(j < NC)
            def _():
                reorder(axis(j), rcv.at[j], canon)
                wd_copy(j).wait()

                def step(at):
                    got = mm_nt(canon[at, :], wdb[lax.rem(j, 2)])

                    @pl.when(j == 0)
                    def _():
                        acc[2, at, :] = got

                    @pl.when(j > 0)
                    def _():
                        acc[2, at, :] += got

                by_rows(step)

                @pl.when(j + 2 < NC)
                def _():
                    wd_copy(j + 2).start()

            @pl.when(j >= NC)
            def _():
                n = j - NC
                reorder(axis(j), rcv.at[j], rcv.at[n])
                for cp in wgu_copies(n):
                    cp.wait()

                def step(at):
                    for m, w in ((0, wgb), (1, wub)):
                        got = mm(rcv[n, at, :], w[lax.rem(n, 2)])

                        @pl.when(n == 0)
                        def _():
                            acc[m, at, :] = got

                        @pl.when(n > 0)
                        def _():
                            acc[m, at, :] += got

                by_rows(step)
                for cp in wgu_copies(n + 2):
                    cp.start()

        @pl.when(i == 0)
        def _():
            for n in range(4, L2):
                ag_second(n)
            for n in range(6, L1):
                ag_first(n)

        @pl.when(i + L1 < 2 * NC)
        def _():
            ag_first(i + L1)

        @pl.when(i + L3 < 2 * NC)
        def _():
            ag_third(i + L3)

        @pl.when(i + L2 < 2 * NC)
        def _():
            ag_second(i + L2)

        return carry

    lax.fori_loop(0, 2 * NC - 1 + LAG, dispatch, 0)

    pl.semaphore_signal(free_sib, inc=1, device_id=sib, device_id_type=MESH)
    for a in range(3):
        for d in (1, 3):
            pl.semaphore_signal(free_ring, inc=1, device_id=frame(a).ring(d), device_id_type=MESH)

    await_once(raux, x_rs.at[2], 15 * MSG)
    await_once(raux, x_self.at[0], MSG)
    await_once(saux, x_ss.at[1], 15 * MSG)
    alane = lax.broadcasted_iota(jnp.int32, (AB, 128), 1)

    def activate(at):
        scale = jnp.sum(jnp.where(alane == me, raux[at, :].astype(F32), 0.0), axis=1, keepdims=True)
        comb = jnp.zeros((AB, 1), F32)
        for half in range(2):
            cols = slice(half * CW, (half + 1) * CW)
            gate, up, back = acc[0, at, cols], acc[1, at, cols], acc[2, at, cols]
            sig = jax.nn.sigmoid(gate)
            act = gate * sig
            comb = comb + jnp.sum(act * up * back, axis=1, keepdims=True)
            scaled = scale * back
            rcv[NC + half, at, :] = (scaled * up * sig * (1.0 + gate * (1.0 - sig))).astype(BF)
            rcv[NC + 2 + half, at, :] = (scaled * act).astype(BF)
        caux[at, :] = jnp.where(alane == me, comb, 0.0).astype(BF)

    def slot_rows(at, n):
        b = lax.rem(n, 2)
        got = mm_nt(rcv[NC, at, :], wgb[b, :, 0:CW])
        got = got + mm_nt(rcv[NC + 1, at, :], wgb[b, :, CW:H])
        got = got + mm_nt(rcv[NC + 2, at, :], wub[b, :, 0:CW])
        got = got + mm_nt(rcv[NC + 3, at, :], wub[b, :, CW:H])
        return got.astype(BF)

    def gain_sum(cut, k, at):
        return jnp.sum(cut.astype(F32) * rcv[k, at, :].astype(F32), axis=0, keepdims=True)

    QB = 4 * MSG
    LAST = 2 * NC - 1
    first_buf = (2 * NC) % NS
    await_spread(rcv.at[LAST], a_rs.at[LAST], a_self.at[LAST])
    for n in (NC - 1, NC):
        for cp in wgu_copies(n):
            cp.wait()
    await_sbuf(first_buf)
    z_mine = rows(zf.place() * MSG, MSG)

    def turn_round(t, gsum):
        du = lax.rem(t + 1, 4)
        u = lax.rem(zf.u + du, 4)
        at = rows(u * QB, QB)
        got = rcv[LAST, at, :]
        rcv[NC - 1, at, :] = got
        acc[0, at, :] += mm(got, wgb[(NC - 1) % 2])
        acc[1, at, :] += mm(got, wub[(NC - 1) % 2])
        for r in range(QB // AB):
            activate(rows(u * QB + r * AB, AB))
        cut = slot_rows(at, NC)
        sbuf[first_buf, at, :] = cut
        for dv in range(4):
            v = lax.rem(zf.v + dv, 4)
            src = sbuf.at[first_buf, rows((u * 4 + v) * MSG, MSG)]
            to = device(*zf.coords(u, v, zf.r), c)
            if dv:
                put(src, tok.at[0, z_mine], a_ss.at[first_buf], r_rs.at[0], to)
            else:

                @pl.when(du != 0)
                def _():
                    put(src, tok.at[0, z_mine], a_ss.at[first_buf], r_rs.at[0], to)

                @pl.when(du == 0)
                def _():
                    pltpu.make_async_copy(src, tok.at[0, z_mine], r_self.at[0]).start()

        return gsum + gain_sum(cut, 0, at)

    gstage[:, 0:CW] = lax.fori_loop(0, 4, turn_round, jnp.zeros((1, CW), F32))
    for n in (NC + 1, NC + 2):
        for cp in wgu_copies(n):
            cp.start()

    half_me, half_sib = rows(c * 512, 512, 512), rows((1 - c) * 512, 512, 512)

    def col_half(k):
        return pl.ds(pl.multiple_of(lax.rem(k, 2) * CW, CW), CW)

    def own_part(k):
        return 2 * lax.div(lax.rem(k, 4), 2)

    def grad_rows(k):
        return rows(lax.div(k, 2) * TOK, TOK, TOK)

    def send_back(i):
        n = i + NC
        a = back_axis(i)
        buf = lax.rem(i + 2 * NC, NS)
        for cp in wgu_copies(n):
            cp.wait()

        def step(r, gsum):
            at = rows(r * RB, RB, RB)
            cut = slot_rows(at, n)
            canon[at, :] = cut
            return gsum + gain_sum(cut, i, at)

        gsum = lax.fori_loop(0, ROWS // RB, step, jnp.zeros((1, CW), F32))
        gstage[:, pl.ds(pl.multiple_of(i * CW, CW), CW)] = gsum
        await_sbuf(buf)
        reorder(a, canon, sbuf.at[buf])
        spread(frame(a), buf, tok.at[i], r_rs.at[i], r_self.at[i])

        @pl.when(i + 2 < NC)
        def _():
            for cp in wgu_copies(n + 2):
                cp.start()

    def combine(k):
        b = lax.rem(k, 2)
        a = back_axis(k)
        await_spread(tok.at[k], r_rs.at[k], r_self.at[k])

        @pl.when(k >= 2)
        def _():
            await_bytes(pbuf.at[b], p_ss.at[b])

        pbuf[b] = mm(gatt[a, half_sib, :], tok[k, 0:ROWS, :]).astype(BF)
        put(pbuf.at[b], tok.at[NC + k, pl.ds(0, 512)], p_ss.at[b], p_rs.at[k], sib)
        acc[own_part(k), 0:512, col_half(k)] = mm(gatt[a, half_me, :], tok[k, 0:ROWS, :])

    def both_cores(k, f, d):
        at = rows(((f.r + d) % 4) * TOK, TOK, TOK)
        return acc[own_part(k), at, col_half(k)] + tok[NC + k, at, :].astype(F32)

    def relay(k):
        b = lax.rem(k, 2)
        f = frame(back_axis(k))
        await_bytes(tok.at[NC + k, pl.ds(0, 512)], p_rs.at[k])

        @pl.when(k >= 2)
        def _():
            await_bytes(q1buf.at[b], q1_ss.at[b])

        q1buf[b] = both_cores(k, f, 2).astype(BF)
        for d, part in ((1, 0), (3, HALF)):
            put(
                q1buf.at[b, pl.ds(part, HALF)], tok.at[NC + k, pl.ds(512 + part, HALF)],
                q1_ss.at[b], q1_rs.at[k], f.ring(d),
            )

    def scatter(k):
        b = lax.rem(k, 2)
        f = frame(back_axis(k))
        await_bytes(tok.at[NC + k, pl.ds(512, TOK)], q1_rs.at[k])

        @pl.when(k >= 2)
        def _():
            await_bytes(q2buf.at[b], q2_ss.at[b])

        on = both_cores(k, f, 1)
        q2buf[b, 0:HALF, :] = (on[0:HALF] + tok[NC + k, 512 : 512 + HALF, :].astype(F32)).astype(BF)
        q2buf[b, HALF:TOK, :] = on[HALF:TOK].astype(BF)
        on = both_cores(k, f, 3)
        q2buf[b, TOK : TOK + HALF, :] = on[0:HALF].astype(BF)
        q2buf[b, TOK + HALF : 2 * TOK, :] = (
            on[HALF:TOK] + tok[NC + k, 512 + HALF : 512 + TOK, :].astype(F32)
        ).astype(BF)
        for d, part in ((1, 0), (3, TOK)):
            put(
                q2buf.at[b, pl.ds(part, TOK)], tok.at[NC + k, pl.ds(640 + part, TOK)],
                q2_ss.at[b], q2_rs.at[k], f.ring(d),
            )
        acc[1, grad_rows(k), col_half(k)] = both_cores(k, f, 0)

    def settle(k):
        await_bytes(tok.at[NC + k, pl.ds(640, 2 * TOK)], q2_rs.at[k])
        grad = acc[1, grad_rows(k), col_half(k)]
        for d in range(2):
            grad = grad + tok[NC + k, 640 + d * TOK : 640 + (d + 1) * TOK, :].astype(F32)
        cols = pl.ds(pl.multiple_of(k * CW, CW), CW)
        scaled = grad * gain[:, cols]
        acc[1, grad_rows(k), col_half(k)] = scaled
        proj_s[...] += scaled * (hid[:, cols].astype(F32) * inv_s[:, 0:1])

    proj_s[...] = jnp.zeros_like(proj_s)

    def back(i, carry):
        @pl.when(i == K1)
        def _():
            pl.semaphore_wait(free_sib, 1)
            pl.semaphore_wait(free_ring, 6)

        @pl.when(jnp.logical_and(i >= 1, i < NC))
        def _():
            send_back(i)

        @pl.when(i >= K4)
        def _():
            settle(i - K4)

        @pl.when(jnp.logical_and(i >= K3, i < NC + K3))
        def _():
            scatter(i - K3)

        @pl.when(jnp.logical_and(i >= K2, i < NC + K2))
        def _():
            relay(i - K2)

        @pl.when(jnp.logical_and(i >= K1, i < NC + K1))
        def _():
            combine(i - K1)

        @pl.when(i == 0)
        def _():
            mine = rows(zf.place() * MSG, MSG)
            for p, d in zf.peers():
                put(caux.at[rows(p * MSG, MSG)], cret.at[mine], x_ss.at[2], x_rs.at[3], d)
            pltpu.make_async_copy(caux.at[mine], cret.at[mine], x_self.at[1]).start()

        @pl.when(i == 3)
        def _():
            await_once(cret, x_rs.at[3], 15 * MSG)
            await_once(cret, x_self.at[1], MSG)
            await_once(caux, x_ss.at[2], 15 * MSG)
            paux[...] = mm(gatt[2, half_sib, :], cret[...]).astype(BF)
            put(paux, sibaux, x_ss.at[3], x_rs.at[4], sib)

        @pl.when(i == 5)
        def _():
            await_bytes(sibaux, x_rs.at[4])
            await_bytes(paux, x_ss.at[3])
            qaux[...] = (mm(gatt[2, half_me, :], cret[...]) + sibaux[...].astype(F32)).astype(BF)
            for d in (1, 2, 3):
                at = rows(((z + d) % 4) * TOK, TOK, TOK)
                put(qaux.at[at], ringaux.at[pl.ds((d - 1) * TOK, TOK)], x_ss.at[4], x_rs.at[5], zf.ring(d))

        @pl.when(i == NC - 1)
        def _():
            gall[zf.place()] = gstage[...]
            for _, d in zf.peers():
                put(gall.at[zf.place()], gall.at[zf.place()], g_ss.at[0], g_rs.at[0], d)

        @pl.when(i == NC)
        def _():
            await_once(gall, g_rs.at[0], 15)
            await_once(gall, g_ss.at[0], 15)
            gring[z] = jnp.sum(gall[...], axis=0)
            for d in (1, 2, 3):
                put(gring.at[z], gring.at[z], g_ss.at[1], g_rs.at[1], zf.ring(d))

        @pl.when(i == NC + 1)
        def _():
            await_once(gring, g_rs.at[1], 3)
            await_once(gring, g_ss.at[1], 3)
            gsib[c] = gring[0] + gring[1] + gring[2] + gring[3]
            put(gsib.at[c], gsib.at[c], g_ss.at[2], g_rs.at[2], sib)

        return carry

    lax.fori_loop(0, NC + K4, back, 0)

    project = jnp.sum(proj_s[...], axis=1, keepdims=True) * (1.0 / D)
    inv = inv_s[:, 0:1]
    for k in range(NC):
        cols = slice(k * CW, (k + 1) * CW)
        scaled = acc[1, (k // 2) * TOK : (k // 2 + 1) * TOK, (k % 2) * CW : (k % 2 + 1) * CW]
        unit = hid[:, cols].astype(F32) * inv
        out_ref[:, cols] = (inv * (scaled - unit * project)).astype(BF)

    await_once(gsib, g_rs.at[2], 1)
    await_once(gsib, g_ss.at[2], 1)
    for r in range(D // 128):
        cols = slice(r * 128, (r + 1) * 128)
        gout_ref[r : r + 1, :] = (gsib[0, :, cols] + gsib[1, :, cols]) / gain[:, cols]

    await_bytes(ringaux, x_rs.at[5])
    await_bytes(ringaux, x_ss.at[4])
    cfin = qaux[rows(z * TOK, TOK, TOK), :].astype(F32)
    for d in range(3):
        cfin = cfin + ringaux[d * TOK : (d + 1) * TOK, :].astype(F32)
    picked = jnp.zeros((TOK, 128), F32)
    named_by = jnp.transpose(turn[...])
    for k in range(4):
        got = jnp.sum(jnp.where(named_by[:, k : k + 1] == lane_f, cfin, 0.0), axis=1, keepdims=True)
        picked = jnp.where(lane == k, got, picked)
    cout_ref[...] = jnp.transpose(picked)[0:4, :].astype(BF)

    for b in range(NS):
        await_sbuf(b)
    for b in range(2):
        await_bytes(pbuf.at[b], p_ss.at[b])
        await_bytes(q1buf.at[b], q1_ss.at[b])
        await_bytes(q2buf.at[b], q2_ss.at[b])


def hand_over(*refs):
    for src, dst in zip(refs[0:3], refs[3:6]):
        dst[...] = src[...]


def shards(hidden_in, norm_gain, upstream, routes, combine_fixed, w_gate, w_up, w_down):
    vm = pl.BlockSpec(memory_space=pltpu.VMEM)
    hbm = pl.BlockSpec(memory_space=pl.ANY)
    dma = pltpu.SemaphoreType.DMA
    shapes = (
        jax.ShapeDtypeStruct((TOK, D), BF),
        jax.ShapeDtypeStruct((D // 128, 128), F32),
        jax.ShapeDtypeStruct((4, TOK), BF),
    )
    results = pl.pallas_call(
        kernel,
        out_shape=shapes,
        in_specs=[hbm, vm, hbm, vm, vm, hbm, hbm, hbm],
        out_specs=(vm, vm, vm),
        scratch_shapes=[
            pltpu.VMEM((2 * NC, GTOK, CW), BF),
            pltpu.VMEM((3, GTOK, 128), BF),
            pltpu.VMEM((3, ROWS, GTOK), BF),
            pltpu.VMEM((3, GTOK, ROWS), BF),
            pltpu.VMEM((2, ROWS, ROWS), BF),
            pltpu.VMEM((NS, ROWS, CW), BF),
            pltpu.VMEM((ROWS, 128), BF),
            pltpu.VMEM((2 * NC, ROWS, CW), BF),
            pltpu.VMEM((ROWS, 128), BF),
            pltpu.VMEM((ROWS, CW), BF),
            pltpu.VMEM((3, ROWS, H), F32),
            pltpu.VMEM((TOK, D), BF),
            pltpu.VMEM((1, D), F32),
            pltpu.VMEM((8, TOK), F32),
            pltpu.VMEM((2, H, CW), BF),
            pltpu.VMEM((2, CW, H), BF),
            pltpu.VMEM((2, CW, H), BF),
            pltpu.VMEM((ROWS, 128), BF),
            pltpu.VMEM((ROWS, 128), BF),
            pltpu.VMEM((2, 512, CW), BF),
            pltpu.VMEM((512, 128), BF),
            pltpu.VMEM((2, TOK, CW), BF),
            pltpu.VMEM((2, 2 * TOK, CW), BF),
            pltpu.VMEM((512, 128), BF),
            pltpu.VMEM((512, 128), BF),
            pltpu.VMEM((384, 128), BF),
            pltpu.VMEM((TOK, 128), F32),
            pltpu.VMEM((TOK, CW), F32),
            pltpu.VMEM((16, 1, D), F32),
            pltpu.VMEM((4, 1, D), F32),
            pltpu.VMEM((2, 1, D), F32),
            pltpu.VMEM((1, D), F32),
            dma((2,)),
            dma((3, 2)),
            dma((2 * NC,)),
            dma((2 * NC,)),
            dma((2 * NC,)),
            dma((2 * NC,)),
            dma((3,)),
            dma((3,)),
            dma((3,)),
            dma((NS,)),
            dma((2 * NC,)),
            dma((2 * NC,)),
            dma((5,)),
            dma((6,)),
            dma((2,)),
            dma((NC,)),
            dma((NC,)),
            dma((2,)),
            dma((NC,)),
            dma((2,)),
            dma((NC,)),
            dma((2,)),
            dma((NC,)),
            dma((3,)),
            dma((3,)),
            pltpu.SemaphoreType.REGULAR,
            pltpu.SemaphoreType.REGULAR,
        ],
        compiler_params=pltpu.CompilerParams(
            collective_id=0, has_side_effects=True, vmem_limit_bytes=63 * 2**20
        ),
        cost_estimate=pl.CostEstimate(flops=50 * 10**9, bytes_accessed=40 * 10**6, transcendentals=10**6),
    )(hidden_in, norm_gain.reshape(D // 128, 128), upstream, routes.T, combine_fixed.T, w_gate, w_up, w_down)
    out, gain_grad, combine_grad = pl.pallas_call(
        hand_over,
        out_shape=shapes,
        in_specs=[vm] * 3,
        out_specs=(vm,) * 3,
    )(*results)
    return out, gain_grad.reshape(D), combine_grad.T


def solution(mesh):
    split = ("expert", "tensor")
    in_specs = (
        P(split, None),
        P(),
        P(split, None),
        P(split, None),
        P(split, None),
        P(split, None, None),
        P(split, None, None),
        P(split, None, None),
    )
    out_specs = (P(split, None), P(), P(split, None))
    return jax.shard_map(shards, mesh=mesh, in_specs=in_specs, out_specs=out_specs, check_vma=False)
```

```python
import jax
import jax.numpy as jnp
from jax import lax
from jax.experimental import pallas as pl
from jax.experimental.pallas import tpu as pltpu
from jax.sharding import PartitionSpec as P

MESH = pl.DeviceIdType.MESH
BF = jnp.bfloat16
F32 = jnp.float32
D = 3584
H = 1024
TOK = 128
CW = 512
NC = D // CW
ROWS = 768
MSG = 48
GTOK = 1024
HALF = TOK // 2
NT = (((1,), (1,)), ((), ()))
PLANE = ((1, 0), (0, 1), (3, 0), (0, 3), (2, 0), (0, 2), (1, 1), (3, 3), (1, 3), (3, 1), (2, 1), (1, 2), (3, 2), (2, 3), (2, 2))
NS = 4
RB = 256
AB = 64
L1, L2, L3 = 7, 5, 3
K1, K2, K3, K4 = 2, 4, 6, 8
LAG = 3


def device(x, y, z, c):
    return {"expert": lax.div(y, 2) * 4 + x, "tensor": z * 4 + lax.rem(y, 2) * 2 + c}


def mm(a, b):
    return jnp.dot(a, b, preferred_element_type=F32)


def mm_nt(a, b):
    return lax.dot_general(a, b, NT, preferred_element_type=F32)


def rows(at, size, align=16):
    return pl.ds(pl.multiple_of(at, align), size)


class Frame:
    def __init__(self, a, x, y, z, c):
        self.is0 = (a - 1) * (a - 2) // 2 if isinstance(a, int) else lax.div((a - 1) * (a - 2), 2)
        self.is1 = a * (2 - a)
        self.is2 = a * (a - 1) // 2 if isinstance(a, int) else lax.div(a * (a - 1), 2)
        self.u = (1 - self.is1) * y + self.is1 * z
        self.v = (1 - self.is0) * x + self.is0 * z
        self.r = self.is2 * z + self.is0 * x + self.is1 * y
        self.c = c

    def coords(self, u, v, r):
        return (
            self.is0 * r + (1 - self.is0) * v,
            self.is1 * r + (1 - self.is1) * u,
            self.is2 * r + self.is0 * v + self.is1 * u,
        )

    def ring(self, d):
        return device(*self.coords(self.u, self.v, lax.rem(self.r + d, 4)), self.c)

    def peers(self):
        for dv, du in PLANE:
            u, v = lax.rem(self.u + du, 4), lax.rem(self.v + dv, 4)
            yield u * 4 + v, device(*self.coords(u, v, self.r), self.c)

    def place(self):
        return self.u * 4 + self.v


def kernel(
    hid_ref, gain_ref, ups_ref, rts_ref, cmb_ref, wg_ref, wu_ref, wd_ref,
    out_ref, gout_ref, cout_ref,
    tok, tokaux, gat, gatt, perm, sbuf, saux, rcv, raux, canon, acc, hid, gain, turn,
    wdb, wgb, wub, caux, cret, pbuf, paux, q1buf, q2buf, qaux, sibaux, ringaux, inv_s, proj_s,
    gall, gring, gsib, gstage,
    i_sem, w_sem, ag_ss, ag_r1, ag_r2, ag_sr, aux_r, aux_s, aux_ss, a_ss, a_rs, a_self, x_ss, x_rs, x_self,
    r_rs, r_self, p_ss, p_rs, q1_ss, q1_rs, q2_ss, q2_rs, g_ss, g_rs, free_sib, free_ring,
):
    e_i, t_i = lax.axis_index("expert"), lax.axis_index("tensor")
    x, y = lax.rem(e_i, 4), lax.div(e_i, 4) * 2 + lax.rem(lax.div(t_i, 2), 2)
    z, c = lax.div(t_i, 4), lax.rem(t_i, 2)
    me = e_i * 16 + t_i
    sib = device(x, y, z, 1 - c)

    def frame(a):
        return Frame(a, x, y, z, c)

    def axis(i):
        return lax.rem(i + 1, 3)

    def back_axis(k):
        return lax.rem(k + 2, 3)

    def own(f):
        return rows((c * 4 + f.r) * TOK, TOK, TOK)

    def ring_rows(f, d):
        return rows((c * 4 + lax.rem(f.r + d, 4)) * TOK, TOK, TOK)

    def put(src, dst, ss, rs, to):
        pltpu.make_async_remote_copy(
            src_ref=src, dst_ref=dst, send_sem=ss, recv_sem=rs, device_id=to, device_id_type=MESH
        ).start()

    def await_bytes(ref, sem):
        pltpu.make_async_copy(ref, ref, sem).wait()

    def await_once(ref, sem, n):
        await_bytes(ref.at[pl.ds(0, n)], sem)

    zf = frame(2)
    bar = pltpu.get_barrier_semaphore()
    everyone = [sib]
    for dx in range(4):
        for dy in range(4):
            for dz in range(4):
                if 0 in (dx, dy, dz) and (dx or dy or dz):
                    everyone.append(device(lax.rem(x + dx, 4), lax.rem(y + dy, 4), lax.rem(z + dz, 4), c))
    for d in everyone:
        pl.semaphore_signal(bar, inc=1, device_id=d, device_id_type=MESH)

    for k in range(NC):
        pltpu.make_async_copy(
            ups_ref.at[:, pl.ds(k * CW, CW)], tok.at[k, own(frame((k + 1) % 3))], i_sem.at[0]
        ).start()
    pltpu.make_async_copy(hid_ref, hid, i_sem.at[1]).start()

    def wd_copy(n):
        return pltpu.make_async_copy(
            wd_ref.at[0, :, pl.ds(pl.multiple_of(n * CW, CW), CW)], wdb.at[lax.rem(n, 2)], w_sem.at[0, lax.rem(n, 2)]
        )

    def wgu_copies(n):
        at = rows(jnp.where(n >= NC, n - NC, n) * CW, CW, CW)
        return (
            pltpu.make_async_copy(wg_ref.at[0, at], wgb.at[lax.rem(n, 2)], w_sem.at[1, lax.rem(n, 2)]),
            pltpu.make_async_copy(wu_ref.at[0, at], wub.at[lax.rem(n, 2)], w_sem.at[2, lax.rem(n, 2)]),
        )

    for n in (0, 1):
        wd_copy(n).start()
        for cp in wgu_copies(n):
            cp.start()

    lane = lax.broadcasted_iota(jnp.int32, (TOK, 128), 1)
    turn[0:4, :] = rts_ref[...].astype(F32)
    turn[4:8, :] = cmb_ref[...].astype(F32) * (1.0 / 65536.0)
    turned = jnp.transpose(turn[...])
    lane_f = lane.astype(F32)
    dense = jnp.zeros((TOK, 128), F32)
    for k in range(4):
        dense = jnp.where(turned[:, k : k + 1] == lane_f, turned[:, 4 + k : 5 + k], dense)
    dense = dense.astype(BF)
    for a in range(3):
        tokaux[a, own(frame(a)), :] = dense
    for r in range(D // 128):
        gain[:, r * 128 : (r + 1) * 128] = gain_ref[r : r + 1, :]

    pl.semaphore_wait(bar, len(everyone))

    for a in (1, 2, 0):
        f = frame(a)
        at = own(f)
        for d in (1, 3, 2):
            put(tokaux.at[a, at], tokaux.at[a, at], aux_ss.at[a], aux_r.at[a], f.ring(d))
        put(tokaux.at[a, at], tokaux.at[a, at], aux_ss.at[a], aux_s.at[a], sib)

    def ag_first(i):
        f = frame(axis(i))
        at = own(f)
        put(tok.at[i, at], tok.at[i, at], ag_ss.at[i], ag_r1.at[i], f.ring(1))
        put(tok.at[i, at], tok.at[i, at], ag_ss.at[i], ag_r1.at[i], f.ring(3))
        put(tok.at[i, at], tok.at[i, at], ag_ss.at[i], ag_sr.at[i], sib)

    def ag_second(i):
        f = frame(axis(i))
        await_once(tok.at[i], ag_r1.at[i], 2 * TOK)
        for d, part in ((3, 0), (1, HALF)):
            at = rows((c * 4 + lax.rem(f.r + d, 4)) * TOK + part, HALF, HALF)
            put(tok.at[i, at], tok.at[i, at], ag_ss.at[i], ag_r2.at[i], f.ring(4 - d))
        for d in (3, 1):
            at = ring_rows(f, d)
            put(tok.at[i, at], tok.at[i, at], ag_ss.at[i], ag_sr.at[i], sib)

    def ag_third(i):
        f = frame(axis(i))
        await_once(tok.at[i], ag_r2.at[i], TOK)
        at = ring_rows(f, 2)
        put(tok.at[i, at], tok.at[i, at], ag_ss.at[i], ag_sr.at[i], sib)

    await_once(tok.at[0], i_sem.at[0], 7 * TOK)
    for i in range(3):
        ag_first(i)

    slot = lax.broadcasted_iota(jnp.int32, (8, ROWS), 1)
    peer = jnp.zeros((8, ROWS), jnp.int32)
    for m in range(1, 16):
        peer = peer + (slot >= MSG * m).astype(jnp.int32)
    rest = slot - MSG * peer
    source = jnp.zeros((8, ROWS), jnp.int32)
    for m in range(1, 8):
        source = source + (rest >= 6 * m).astype(jnp.int32)
    place = rest - 6 * source
    pu, pv = lax.shift_right_logical(peer, 2), lax.bitwise_and(peer, 3)
    sc, sr = lax.shift_right_logical(source, 2), lax.bitwise_and(source, 3)

    def build(a):
        f = frame(a)
        await_once(tokaux.at[a], aux_s.at[a], 4 * TOK)
        await_once(tokaux.at[a], aux_ss.at[a], 7 * TOK)
        px, py, pz = f.coords(pu, pv, jnp.zeros_like(pu) + f.r)
        expert = (
            (lax.shift_right_logical(py, 1) * 4 + px) * 16 + pz * 4 + lax.bitwise_and(py, 1) * 2 + c
        )
        pick = (
            lax.broadcasted_iota(jnp.int32, (128, ROWS), 0) == jnp.broadcast_to(expert[0:1], (128, ROWS))
        ).astype(F32).astype(BF)
        below = (
            lax.broadcasted_iota(jnp.int32, (TOK, TOK), 0) > lax.broadcasted_iota(jnp.int32, (TOK, TOK), 1)
        ).astype(F32).astype(BF)
        for s in range(8):
            part = slice(s * TOK, (s + 1) * TOK)
            named = (tokaux[a, part, :].astype(F32) != 0.0).astype(F32)
            code = (mm(below, named.astype(BF)) + 1.0) * named
            want = jnp.where(source[0:1] == s, (place[0:1] + 1).astype(F32), -1.0)
            hot = (mm(code.astype(BF), pick) == jnp.broadcast_to(want, (TOK, ROWS))).astype(F32)
            gatt[a, part, :] = hot.astype(BF)
            gat[a, :, part] = jnp.transpose(hot).astype(BF)

    def swaps():
        swap_x = (pu * 4 + sr) * MSG + (sc * 4 + pv) * 6 + place
        swap_y = (sr * 4 + pv) * MSG + (sc * 4 + pu) * 6 + place
        at = lax.broadcasted_iota(jnp.int32, (ROWS, ROWS), 0)
        for a, to in ((0, swap_x), (1, swap_y)):
            perm[a] = (at == jnp.broadcast_to(to[0:1], (ROWS, ROWS))).astype(F32).astype(BF)

    def norm():
        await_bytes(hid, i_sem.at[1])
        total = jnp.zeros((TOK, CW), F32)
        for k in range(NC):
            h = hid[:, k * CW : (k + 1) * CW].astype(F32)
            total = total + h * h
        inv = lax.rsqrt(jnp.sum(total, axis=1, keepdims=True) * (1.0 / D) + 1e-06)
        inv_s[...] = jnp.broadcast_to(inv, (TOK, 128))
        for k in range(NC):
            cols = slice(k * CW, (k + 1) * CW)
            unit = hid[:, cols].astype(F32) * inv
            tok[NC + k, own(frame((NC + k + 1) % 3)), :] = (unit * gain[:, cols]).astype(BF)

    norm()
    for a in (1, 2, 0):
        f = frame(a)
        await_once(tokaux.at[a], aux_r.at[a], 3 * TOK)
        for d in (1, 3, 2):
            at = ring_rows(f, d)
            put(tokaux.at[a, at], tokaux.at[a, at], aux_ss.at[a], aux_s.at[a], sib)
    for i in range(3):
        ag_second(i)
    build(1)
    for i in range(3):
        ag_third(i)
    for i in range(3, 6):
        ag_first(i)
    swaps()
    ag_second(3)

    def spread(f, buf, dst, rs, self_sem):
        mine = rows(f.place() * MSG, MSG)
        for p, d in f.peers():
            put(sbuf.at[buf, rows(p * MSG, MSG)], dst.at[mine], a_ss.at[buf], rs, d)
        pltpu.make_async_copy(sbuf.at[buf, mine], dst.at[mine], self_sem).start()

    def await_spread(dst, rs, self_sem):
        await_once(dst, rs, 15 * MSG)
        await_once(dst, self_sem, MSG)

    def await_sbuf(buf):
        await_once(sbuf.at[buf], a_ss.at[buf], 15 * MSG)

    def by_rows(step):
        def body(r, cc):
            step(rows(r * RB, RB, RB))
            return cc

        lax.fori_loop(0, ROWS // RB, body, 0)

    def reorder(a, src, dst):
        @pl.when(a == 2)
        def _():
            dst[...] = src[...]

        @pl.when(a != 2)
        def _():
            def step(at):
                dst[at, :] = mm(perm[jnp.minimum(a, 1), at, :], src[...]).astype(BF)

            by_rows(step)

    def dispatch(i, carry):
        @pl.when(i < 2 * NC)
        def _():
            buf = lax.rem(i, NS)
            a = axis(i)

            @pl.when(jnp.logical_and(i >= 1, i < 3))
            def _():
                build(a)

            await_once(tok.at[i], ag_sr.at[i], 4 * TOK)

            @pl.when(i >= NS)
            def _():
                await_sbuf(buf)

            def gather(at):
                sbuf[buf, at, :] = mm(gat[a, at, :], tok[i]).astype(BF)

            by_rows(gather)
            await_once(tok.at[i], ag_ss.at[i], 7 * TOK)
            spread(frame(a), buf, rcv.at[i], a_rs.at[i], a_self.at[i])

        @pl.when(i == 1)
        def _():
            saux[...] = mm(gat[2], tokaux[2]).astype(BF)
            mine = rows(zf.place() * MSG, MSG)
            for p, d in zf.peers():
                put(saux.at[rows(p * MSG, MSG)], raux.at[mine], x_ss.at[1], x_rs.at[2], d)
            pltpu.make_async_copy(saux.at[mine], raux.at[mine], x_self.at[0]).start()

        @pl.when(i >= LAG)
        def _():
            j = i - LAG
            await_spread(rcv.at[j], a_rs.at[j], a_self.at[j])

            @pl.when(j < NC)
            def _():
                reorder(axis(j), rcv.at[j], canon)
                wd_copy(j).wait()

                def step(at):
                    got = mm_nt(canon[at, :], wdb[lax.rem(j, 2)])

                    @pl.when(j == 0)
                    def _():
                        acc[2, at, :] = got

                    @pl.when(j > 0)
                    def _():
                        acc[2, at, :] += got

                by_rows(step)

                @pl.when(j + 2 < NC)
                def _():
                    wd_copy(j + 2).start()

            @pl.when(j >= NC)
            def _():
                n = j - NC
                reorder(axis(j), rcv.at[j], rcv.at[n])
                for cp in wgu_copies(n):
                    cp.wait()

                def step(at):
                    for m, w in ((0, wgb), (1, wub)):
                        got = mm(rcv[n, at, :], w[lax.rem(n, 2)])

                        @pl.when(n == 0)
                        def _():
                            acc[m, at, :] = got

                        @pl.when(n > 0)
                        def _():
                            acc[m, at, :] += got

                by_rows(step)
                for cp in wgu_copies(n + 2):
                    cp.start()

        @pl.when(i == 0)
        def _():
            for n in range(4, L2):
                ag_second(n)
            for n in range(6, L1):
                ag_first(n)

        @pl.when(i + L1 < 2 * NC)
        def _():
            ag_first(i + L1)

        @pl.when(i + L3 < 2 * NC)
        def _():
            ag_third(i + L3)

        @pl.when(i + L2 < 2 * NC)
        def _():
            ag_second(i + L2)

        return carry

    lax.fori_loop(0, 2 * NC - 1 + LAG, dispatch, 0)

    pl.semaphore_signal(free_sib, inc=1, device_id=sib, device_id_type=MESH)
    for a in range(3):
        for d in (1, 3):
            pl.semaphore_signal(free_ring, inc=1, device_id=frame(a).ring(d), device_id_type=MESH)

    await_once(raux, x_rs.at[2], 15 * MSG)
    await_once(raux, x_self.at[0], MSG)
    await_once(saux, x_ss.at[1], 15 * MSG)
    alane = lax.broadcasted_iota(jnp.int32, (AB, 128), 1)

    def activate(at):
        scale = jnp.sum(jnp.where(alane == me, raux[at, :].astype(F32), 0.0), axis=1, keepdims=True)
        comb = jnp.zeros((AB, 1), F32)
        for half in range(2):
            cols = slice(half * CW, (half + 1) * CW)
            gate, up, back = acc[0, at, cols], acc[1, at, cols], acc[2, at, cols]
            sig = jax.nn.sigmoid(gate)
            act = gate * sig
            comb = comb + jnp.sum(act * up * back, axis=1, keepdims=True)
            scaled = scale * back
            rcv[NC + half, at, :] = (scaled * up * sig * (1.0 + gate * (1.0 - sig))).astype(BF)
            rcv[NC + 2 + half, at, :] = (scaled * act).astype(BF)
        caux[at, :] = jnp.where(alane == me, comb, 0.0).astype(BF)

    def slot_rows(at, n):
        b = lax.rem(n, 2)
        got = mm_nt(rcv[NC, at, :], wgb[b, :, 0:CW])
        got = got + mm_nt(rcv[NC + 1, at, :], wgb[b, :, CW:H])
        got = got + mm_nt(rcv[NC + 2, at, :], wub[b, :, 0:CW])
        got = got + mm_nt(rcv[NC + 3, at, :], wub[b, :, CW:H])
        return got.astype(BF)

    def gain_sum(cut, k, at):
        return jnp.sum(cut.astype(F32) * rcv[k, at, :].astype(F32), axis=0, keepdims=True)

    QB = 4 * MSG
    LAST = 2 * NC - 1
    first_buf = (2 * NC) % NS
    await_spread(rcv.at[LAST], a_rs.at[LAST], a_self.at[LAST])
    for n in (NC - 1, NC):
        for cp in wgu_copies(n):
            cp.wait()
    await_sbuf(first_buf)
    z_mine = rows(zf.place() * MSG, MSG)

    def turn_round(t, gsum):
        du = lax.rem(t + 1, 4)
        u = lax.rem(zf.u + du, 4)
        at = rows(u * QB, QB)
        got = rcv[LAST, at, :]
        rcv[NC - 1, at, :] = got
        acc[0, at, :] += mm(got, wgb[(NC - 1) % 2])
        acc[1, at, :] += mm(got, wub[(NC - 1) % 2])
        for r in range(QB // AB):
            activate(rows(u * QB + r * AB, AB))
        cut = slot_rows(at, NC)
        sbuf[first_buf, at, :] = cut
        for dv in range(4):
            v = lax.rem(zf.v + dv, 4)
            src = sbuf.at[first_buf, rows((u * 4 + v) * MSG, MSG)]
            to = device(*zf.coords(u, v, zf.r), c)
            if dv:
                put(src, tok.at[0, z_mine], a_ss.at[first_buf], r_rs.at[0], to)
            else:

                @pl.when(du != 0)
                def _():
                    put(src, tok.at[0, z_mine], a_ss.at[first_buf], r_rs.at[0], to)

                @pl.when(du == 0)
                def _():
                    pltpu.make_async_copy(src, tok.at[0, z_mine], r_self.at[0]).start()

        return gsum + gain_sum(cut, 0, at)

    gstage[:, 0:CW] = lax.fori_loop(0, 4, turn_round, jnp.zeros((1, CW), F32))
    for n in (NC + 1, NC + 2):
        for cp in wgu_copies(n):
            cp.start()

    half_me, half_sib = rows(c * 512, 512, 512), rows((1 - c) * 512, 512, 512)

    def col_half(k):
        return pl.ds(pl.multiple_of(lax.rem(k, 2) * CW, CW), CW)

    def own_part(k):
        return 2 * lax.div(lax.rem(k, 4), 2)

    def grad_rows(k):
        return rows(lax.div(k, 2) * TOK, TOK, TOK)

    def send_back(i):
        n = i + NC
        a = back_axis(i)
        buf = lax.rem(i + 2 * NC, NS)
        for cp in wgu_copies(n):
            cp.wait()

        def step(r, gsum):
            at = rows(r * RB, RB, RB)
            cut = slot_rows(at, n)
            canon[at, :] = cut
            return gsum + gain_sum(cut, i, at)

        gsum = lax.fori_loop(0, ROWS // RB, step, jnp.zeros((1, CW), F32))
        gstage[:, pl.ds(pl.multiple_of(i * CW, CW), CW)] = gsum
        await_sbuf(buf)
        reorder(a, canon, sbuf.at[buf])
        spread(frame(a), buf, tok.at[i], r_rs.at[i], r_self.at[i])

        @pl.when(i + 2 < NC)
        def _():
            for cp in wgu_copies(n + 2):
                cp.start()

    def combine(k):
        b = lax.rem(k, 2)
        a = back_axis(k)
        await_spread(tok.at[k], r_rs.at[k], r_self.at[k])

        @pl.when(k >= 2)
        def _():
            await_bytes(pbuf.at[b], p_ss.at[b])

        pbuf[b] = mm(gatt[a, half_sib, :], tok[k, 0:ROWS, :]).astype(BF)
        put(pbuf.at[b], tok.at[NC + k, pl.ds(0, 512)], p_ss.at[b], p_rs.at[k], sib)
        acc[own_part(k), 0:512, col_half(k)] = mm(gatt[a, half_me, :], tok[k, 0:ROWS, :])

    def both_cores(k, f, d):
        at = rows(lax.rem(f.r + d, 4) * TOK, TOK, TOK)
        return acc[own_part(k), at, col_half(k)] + tok[NC + k, at, :].astype(F32)

    def relay(k):
        b = lax.rem(k, 2)
        f = frame(back_axis(k))
        await_bytes(tok.at[NC + k, pl.ds(0, 512)], p_rs.at[k])

        @pl.when(k >= 2)
        def _():
            await_bytes(q1buf.at[b], q1_ss.at[b])

        q1buf[b] = both_cores(k, f, 2).astype(BF)
        for d, part in ((1, 0), (3, HALF)):
            put(
                q1buf.at[b, pl.ds(part, HALF)], tok.at[NC + k, pl.ds(512 + part, HALF)],
                q1_ss.at[b], q1_rs.at[k], f.ring(d),
            )

    def scatter(k):
        b = lax.rem(k, 2)
        f = frame(back_axis(k))
        await_bytes(tok.at[NC + k, pl.ds(512, TOK)], q1_rs.at[k])

        @pl.when(k >= 2)
        def _():
            await_bytes(q2buf.at[b], q2_ss.at[b])

        on = both_cores(k, f, 1)
        q2buf[b, 0:HALF, :] = (on[0:HALF] + tok[NC + k, 512 : 512 + HALF, :].astype(F32)).astype(BF)
        q2buf[b, HALF:TOK, :] = on[HALF:TOK].astype(BF)
        on = both_cores(k, f, 3)
        q2buf[b, TOK : TOK + HALF, :] = on[0:HALF].astype(BF)
        q2buf[b, TOK + HALF : 2 * TOK, :] = (
            on[HALF:TOK] + tok[NC + k, 512 + HALF : 512 + TOK, :].astype(F32)
        ).astype(BF)
        for d, part in ((1, 0), (3, TOK)):
            put(
                q2buf.at[b, pl.ds(part, TOK)], tok.at[NC + k, pl.ds(640 + part, TOK)],
                q2_ss.at[b], q2_rs.at[k], f.ring(d),
            )
        acc[1, grad_rows(k), col_half(k)] = both_cores(k, f, 0)

    def settle(k):
        await_bytes(tok.at[NC + k, pl.ds(640, 2 * TOK)], q2_rs.at[k])
        grad = acc[1, grad_rows(k), col_half(k)]
        for d in range(2):
            grad = grad + tok[NC + k, 640 + d * TOK : 640 + (d + 1) * TOK, :].astype(F32)
        cols = pl.ds(pl.multiple_of(k * CW, CW), CW)
        scaled = grad * gain[:, cols]
        acc[1, grad_rows(k), col_half(k)] = scaled
        proj_s[...] += scaled * (hid[:, cols].astype(F32) * inv_s[:, 0:1])

    proj_s[...] = jnp.zeros_like(proj_s)

    def back(i, carry):
        @pl.when(i == K1)
        def _():
            pl.semaphore_wait(free_sib, 1)
            pl.semaphore_wait(free_ring, 6)

        @pl.when(jnp.logical_and(i >= 1, i < NC))
        def _():
            send_back(i)

        @pl.when(i >= K4)
        def _():
            settle(i - K4)

        @pl.when(jnp.logical_and(i >= K3, i < NC + K3))
        def _():
            scatter(i - K3)

        @pl.when(jnp.logical_and(i >= K2, i < NC + K2))
        def _():
            relay(i - K2)

        @pl.when(jnp.logical_and(i >= K1, i < NC + K1))
        def _():
            combine(i - K1)

        @pl.when(i == 0)
        def _():
            mine = rows(zf.place() * MSG, MSG)
            for p, d in zf.peers():
                put(caux.at[rows(p * MSG, MSG)], cret.at[mine], x_ss.at[2], x_rs.at[3], d)
            pltpu.make_async_copy(caux.at[mine], cret.at[mine], x_self.at[1]).start()

        @pl.when(i == 3)
        def _():
            await_once(cret, x_rs.at[3], 15 * MSG)
            await_once(cret, x_self.at[1], MSG)
            await_once(caux, x_ss.at[2], 15 * MSG)
            paux[...] = mm(gatt[2, half_sib, :], cret[...]).astype(BF)
            put(paux, sibaux, x_ss.at[3], x_rs.at[4], sib)

        @pl.when(i == 5)
        def _():
            await_bytes(sibaux, x_rs.at[4])
            await_bytes(paux, x_ss.at[3])
            qaux[...] = (mm(gatt[2, half_me, :], cret[...]) + sibaux[...].astype(F32)).astype(BF)
            for d in (1, 2, 3):
                at = rows(((z + d) % 4) * TOK, TOK, TOK)
                put(qaux.at[at], ringaux.at[pl.ds((d - 1) * TOK, TOK)], x_ss.at[4], x_rs.at[5], zf.ring(d))

        @pl.when(i == NC - 1)
        def _():
            gall[zf.place()] = gstage[...]
            for _, d in zf.peers():
                put(gall.at[zf.place()], gall.at[zf.place()], g_ss.at[0], g_rs.at[0], d)

        @pl.when(i == NC)
        def _():
            await_once(gall, g_rs.at[0], 15)
            await_once(gall, g_ss.at[0], 15)
            gring[z] = jnp.sum(gall[...], axis=0)
            for d in (1, 2, 3):
                put(gring.at[z], gring.at[z], g_ss.at[1], g_rs.at[1], zf.ring(d))

        @pl.when(i == NC + 1)
        def _():
            await_once(gring, g_rs.at[1], 3)
            await_once(gring, g_ss.at[1], 3)
            gsib[c] = gring[0] + gring[1] + gring[2] + gring[3]
            put(gsib.at[c], gsib.at[c], g_ss.at[2], g_rs.at[2], sib)

        return carry

    lax.fori_loop(0, NC + K4, back, 0)

    project = jnp.sum(proj_s[...], axis=1, keepdims=True) * (1.0 / D)
    inv = inv_s[:, 0:1]
    for k in range(NC):
        cols = slice(k * CW, (k + 1) * CW)
        scaled = acc[1, (k // 2) * TOK : (k // 2 + 1) * TOK, (k % 2) * CW : (k % 2 + 1) * CW]
        unit = hid[:, cols].astype(F32) * inv
        out_ref[:, cols] = (inv * (scaled - unit * project)).astype(BF)

    await_once(gsib, g_rs.at[2], 1)
    await_once(gsib, g_ss.at[2], 1)
    for r in range(D // 128):
        cols = slice(r * 128, (r + 1) * 128)
        gout_ref[r : r + 1, :] = (gsib[0, :, cols] + gsib[1, :, cols]) / gain[:, cols]

    await_bytes(ringaux, x_rs.at[5])
    await_bytes(ringaux, x_ss.at[4])
    cfin = qaux[rows(z * TOK, TOK, TOK), :].astype(F32)
    for d in range(3):
        cfin = cfin + ringaux[d * TOK : (d + 1) * TOK, :].astype(F32)
    picked = jnp.zeros((TOK, 128), F32)
    named_by = jnp.transpose(turn[...])
    for k in range(4):
        got = jnp.sum(jnp.where(named_by[:, k : k + 1] == lane_f, cfin, 0.0), axis=1, keepdims=True)
        picked = jnp.where(lane == k, got, picked)
    cout_ref[...] = jnp.transpose(picked)[0:4, :].astype(BF)

    for b in range(NS):
        await_sbuf(b)
    for b in range(2):
        await_bytes(pbuf.at[b], p_ss.at[b])
        await_bytes(q1buf.at[b], q1_ss.at[b])
        await_bytes(q2buf.at[b], q2_ss.at[b])


def hand_over(*refs):
    for src, dst in zip(refs[0:3], refs[3:6]):
        dst[...] = src[...]


def shards(hidden_in, norm_gain, upstream, routes, combine_fixed, w_gate, w_up, w_down):
    vm = pl.BlockSpec(memory_space=pltpu.VMEM)
    hbm = pl.BlockSpec(memory_space=pl.ANY)
    dma = pltpu.SemaphoreType.DMA
    shapes = (
        jax.ShapeDtypeStruct((TOK, D), BF),
        jax.ShapeDtypeStruct((D // 128, 128), F32),
        jax.ShapeDtypeStruct((4, TOK), BF),
    )
    results = pl.pallas_call(
        kernel,
        out_shape=shapes,
        in_specs=[hbm, vm, hbm, vm, vm, hbm, hbm, hbm],
        out_specs=(vm, vm, vm),
        scratch_shapes=[
            pltpu.VMEM((2 * NC, GTOK, CW), BF),
            pltpu.VMEM((3, GTOK, 128), BF),
            pltpu.VMEM((3, ROWS, GTOK), BF),
            pltpu.VMEM((3, GTOK, ROWS), BF),
            pltpu.VMEM((2, ROWS, ROWS), BF),
            pltpu.VMEM((NS, ROWS, CW), BF),
            pltpu.VMEM((ROWS, 128), BF),
            pltpu.VMEM((2 * NC, ROWS, CW), BF),
            pltpu.VMEM((ROWS, 128), BF),
            pltpu.VMEM((ROWS, CW), BF),
            pltpu.VMEM((3, ROWS, H), F32),
            pltpu.VMEM((TOK, D), BF),
            pltpu.VMEM((1, D), F32),
            pltpu.VMEM((8, TOK), F32),
            pltpu.VMEM((2, H, CW), BF),
            pltpu.VMEM((2, CW, H), BF),
            pltpu.VMEM((2, CW, H), BF),
            pltpu.VMEM((ROWS, 128), BF),
            pltpu.VMEM((ROWS, 128), BF),
            pltpu.VMEM((2, 512, CW), BF),
            pltpu.VMEM((512, 128), BF),
            pltpu.VMEM((2, TOK, CW), BF),
            pltpu.VMEM((2, 2 * TOK, CW), BF),
            pltpu.VMEM((512, 128), BF),
            pltpu.VMEM((512, 128), BF),
            pltpu.VMEM((384, 128), BF),
            pltpu.VMEM((TOK, 128), F32),
            pltpu.VMEM((TOK, CW), F32),
            pltpu.VMEM((16, 1, D), F32),
            pltpu.VMEM((4, 1, D), F32),
            pltpu.VMEM((2, 1, D), F32),
            pltpu.VMEM((1, D), F32),
            dma((2,)),
            dma((3, 2)),
            dma((2 * NC,)),
            dma((2 * NC,)),
            dma((2 * NC,)),
            dma((2 * NC,)),
            dma((3,)),
            dma((3,)),
            dma((3,)),
            dma((NS,)),
            dma((2 * NC,)),
            dma((2 * NC,)),
            dma((5,)),
            dma((6,)),
            dma((2,)),
            dma((NC,)),
            dma((NC,)),
            dma((2,)),
            dma((NC,)),
            dma((2,)),
            dma((NC,)),
            dma((2,)),
            dma((NC,)),
            dma((3,)),
            dma((3,)),
            pltpu.SemaphoreType.REGULAR,
            pltpu.SemaphoreType.REGULAR,
        ],
        compiler_params=pltpu.CompilerParams(
            collective_id=0, has_side_effects=True, vmem_limit_bytes=63 * 2**20
        ),
        cost_estimate=pl.CostEstimate(flops=50 * 10**9, bytes_accessed=40 * 10**6, transcendentals=10**6),
    )(hidden_in, norm_gain.reshape(D // 128, 128), upstream, routes.T, combine_fixed.T, w_gate, w_up, w_down)
    out, gain_grad, combine_grad = pl.pallas_call(
        hand_over,
        out_shape=shapes,
        in_specs=[vm] * 3,
        out_specs=(vm,) * 3,
    )(*results)
    return out, gain_grad.reshape(D), combine_grad.T


def solution(mesh):
    split = ("expert", "tensor")
    in_specs = (
        P(split, None),
        P(),
        P(split, None),
        P(split, None),
        P(split, None),
        P(split, None, None),
        P(split, None, None),
        P(split, None, None),
    )
    out_specs = (P(split, None), P(), P(split, None))
    return jax.shard_map(shards, mesh=mesh, in_specs=in_specs, out_specs=out_specs, check_vma=False)
```

```python
import jax
import jax.numpy as jnp
from jax import lax
from jax.experimental import pallas as pl
from jax.experimental.pallas import tpu as pltpu
from jax.sharding import PartitionSpec as P

MESH = pl.DeviceIdType.MESH
BF = jnp.bfloat16
F32 = jnp.float32
D = 3584
H = 1024
TOK = 128
CW = 512
NC = D // CW
ROWS = 768
MSG = 48
GTOK = 1024
HALF = TOK // 2
NT = (((1,), (1,)), ((), ()))
PLANE = ((1, 0), (0, 1), (3, 0), (0, 3), (2, 0), (0, 2), (1, 1), (3, 3), (1, 3), (3, 1), (2, 1), (1, 2), (3, 2), (2, 3), (2, 2))
NS = 4
RB = 256
AB = 64
L1, L2, L3 = 7, 5, 3
K1, K2, K3, K4 = 2, 4, 6, 8
LAG = 3


def device(x, y, z, c):
    return {"expert": lax.div(y, 2) * 4 + x, "tensor": z * 4 + lax.rem(y, 2) * 2 + c}


def mm(a, b):
    return jnp.dot(a, b, preferred_element_type=F32)


def mm_nt(a, b):
    return lax.dot_general(a, b, NT, preferred_element_type=F32)


def rows(at, size, align=16):
    return pl.ds(pl.multiple_of(at, align), size)


class Frame:
    def __init__(self, a, x, y, z, c):
        self.is0 = (a - 1) * (a - 2) // 2 if isinstance(a, int) else lax.div((a - 1) * (a - 2), 2)
        self.is1 = a * (2 - a)
        self.is2 = a * (a - 1) // 2 if isinstance(a, int) else lax.div(a * (a - 1), 2)
        self.u = (1 - self.is1) * y + self.is1 * z
        self.v = (1 - self.is0) * x + self.is0 * z
        self.r = self.is2 * z + self.is0 * x + self.is1 * y
        self.c = c

    def coords(self, u, v, r):
        return (
            self.is0 * r + (1 - self.is0) * v,
            self.is1 * r + (1 - self.is1) * u,
            self.is2 * r + self.is0 * v + self.is1 * u,
        )

    def ring(self, d):
        return device(*self.coords(self.u, self.v, lax.rem(self.r + d, 4)), self.c)

    def peers(self):
        for dv, du in PLANE:
            u, v = lax.rem(self.u + du, 4), lax.rem(self.v + dv, 4)
            yield u * 4 + v, device(*self.coords(u, v, self.r), self.c)

    def place(self):
        return self.u * 4 + self.v


def kernel(
    hid_ref, gain_ref, ups_ref, rts_ref, cmb_ref, wg_ref, wu_ref, wd_ref,
    out_ref, gout_ref, cout_ref,
    tok, tokaux, gat, gatt, perm, sbuf, saux, rcv, raux, canon, acc, hid, gain, turn,
    wdb, wgb, wub, caux, cret, pbuf, paux, q1buf, q2buf, qaux, sibaux, ringaux, inv_s, proj_s,
    gall, gring, gsib, gstage,
    i_sem, w_sem, ag_ss, ag_r1, ag_r2, ag_sr, aux_r, aux_s, aux_ss, a_ss, a_rs, a_self, x_ss, x_rs, x_self,
    r_rs, r_self, p_ss, p_rs, q1_ss, q1_rs, q2_ss, q2_rs, g_ss, g_rs, free_sib, free_ring,
):
    e_i, t_i = lax.axis_index("expert"), lax.axis_index("tensor")
    x, y = lax.rem(e_i, 4), lax.div(e_i, 4) * 2 + lax.rem(lax.div(t_i, 2), 2)
    z, c = lax.div(t_i, 4), lax.rem(t_i, 2)
    me = e_i * 16 + t_i
    sib = device(x, y, z, 1 - c)

    def frame(a):
        return Frame(a, x, y, z, c)

    def axis(i):
        return lax.rem(i + 1, 3)

    def back_axis(k):
        return lax.rem(k + 2, 3)

    def own(f):
        return rows((c * 4 + f.r) * TOK, TOK, TOK)

    def ring_rows(f, d):
        return rows((c * 4 + lax.rem(f.r + d, 4)) * TOK, TOK, TOK)

    def put(src, dst, ss, rs, to):
        pltpu.make_async_remote_copy(
            src_ref=src, dst_ref=dst, send_sem=ss, recv_sem=rs, device_id=to, device_id_type=MESH
        ).start()

    def await_bytes(ref, sem):
        pltpu.make_async_copy(ref, ref, sem).wait()

    def await_once(ref, sem, n):
        await_bytes(ref.at[pl.ds(0, n)], sem)

    zf = frame(2)
    bar = pltpu.get_barrier_semaphore()
    everyone = [sib]
    for dx in range(4):
        for dy in range(4):
            for dz in range(4):
                if 0 in (dx, dy, dz) and (dx or dy or dz):
                    everyone.append(device(lax.rem(x + dx, 4), lax.rem(y + dy, 4), lax.rem(z + dz, 4), c))
    for d in everyone:
        pl.semaphore_signal(bar, inc=1, device_id=d, device_id_type=MESH)

    for k in range(NC):
        pltpu.make_async_copy(
            ups_ref.at[:, pl.ds(k * CW, CW)], tok.at[k, own(frame((k + 1) % 3))], i_sem.at[0]
        ).start()
    pltpu.make_async_copy(hid_ref, hid, i_sem.at[1]).start()

    def wd_copy(n):
        return pltpu.make_async_copy(
            wd_ref.at[0, :, pl.ds(pl.multiple_of(n * CW, CW), CW)], wdb.at[lax.rem(n, 2)], w_sem.at[0, lax.rem(n, 2)]
        )

    def wgu_copies(n):
        at = rows(jnp.where(n >= NC, n - NC, n) * CW, CW, CW)
        return (
            pltpu.make_async_copy(wg_ref.at[0, at], wgb.at[lax.rem(n, 2)], w_sem.at[1, lax.rem(n, 2)]),
            pltpu.make_async_copy(wu_ref.at[0, at], wub.at[lax.rem(n, 2)], w_sem.at[2, lax.rem(n, 2)]),
        )

    for n in (0, 1):
        wd_copy(n).start()
        for cp in wgu_copies(n):
            cp.start()

    lane = lax.broadcasted_iota(jnp.int32, (TOK, 128), 1)
    turn[0:4, :] = rts_ref[...].astype(F32)
    turn[4:8, :] = cmb_ref[...].astype(F32) * (1.0 / 65536.0)
    turned = jnp.transpose(turn[...])
    lane_f = lane.astype(F32)
    dense = jnp.zeros((TOK, 128), F32)
    for k in range(4):
        dense = jnp.where(turned[:, k : k + 1] == lane_f, turned[:, 4 + k : 5 + k], dense)
    dense = dense.astype(BF)
    for a in range(3):
        tokaux[a, own(frame(a)), :] = dense
    for r in range(D // 128):
        gain[:, r * 128 : (r + 1) * 128] = gain_ref[r : r + 1, :]

    pl.semaphore_wait(bar, len(everyone))

    for a in (1, 2, 0):
        f = frame(a)
        at = own(f)
        for d in (1, 3, 2):
            put(tokaux.at[a, at], tokaux.at[a, at], aux_ss.at[a], aux_r.at[a], f.ring(d))
        put(tokaux.at[a, at], tokaux.at[a, at], aux_ss.at[a], aux_s.at[a], sib)

    def ag_first(i):
        f = frame(axis(i))
        at = own(f)
        put(tok.at[i, at], tok.at[i, at], ag_ss.at[i], ag_r1.at[i], f.ring(1))
        put(tok.at[i, at], tok.at[i, at], ag_ss.at[i], ag_r1.at[i], f.ring(3))
        put(tok.at[i, at], tok.at[i, at], ag_ss.at[i], ag_sr.at[i], sib)

    def ag_second(i):
        f = frame(axis(i))
        await_once(tok.at[i], ag_r1.at[i], 2 * TOK)
        for d, part in ((3, 0), (1, HALF)):
            at = rows((c * 4 + lax.rem(f.r + d, 4)) * TOK + part, HALF, HALF)
            put(tok.at[i, at], tok.at[i, at], ag_ss.at[i], ag_r2.at[i], f.ring(4 - d))
        for d in (3, 1):
            at = ring_rows(f, d)
            put(tok.at[i, at], tok.at[i, at], ag_ss.at[i], ag_sr.at[i], sib)

    def ag_third(i):
        f = frame(axis(i))
        await_once(tok.at[i], ag_r2.at[i], TOK)
        at = ring_rows(f, 2)
        put(tok.at[i, at], tok.at[i, at], ag_ss.at[i], ag_sr.at[i], sib)

    await_once(tok.at[0], i_sem.at[0], 7 * TOK)
    for i in range(3):
        ag_first(i)

    slot = lax.broadcasted_iota(jnp.int32, (8, ROWS), 1)
    peer = jnp.zeros((8, ROWS), jnp.int32)
    for m in range(1, 16):
        peer = peer + (slot >= MSG * m).astype(jnp.int32)
    rest = slot - MSG * peer
    source = jnp.zeros((8, ROWS), jnp.int32)
    for m in range(1, 8):
        source = source + (rest >= 6 * m).astype(jnp.int32)
    place = rest - 6 * source
    pu, pv = lax.shift_right_logical(peer, 2), lax.bitwise_and(peer, 3)
    sc, sr = lax.shift_right_logical(source, 2), lax.bitwise_and(source, 3)

    def build(a):
        f = frame(a)
        await_once(tokaux.at[a], aux_s.at[a], 4 * TOK)
        await_once(tokaux.at[a], aux_ss.at[a], 7 * TOK)
        px, py, pz = f.coords(pu, pv, jnp.zeros_like(pu) + f.r)
        expert = (
            (lax.shift_right_logical(py, 1) * 4 + px) * 16 + pz * 4 + lax.bitwise_and(py, 1) * 2 + c
        )
        pick = (
            lax.broadcasted_iota(jnp.int32, (128, ROWS), 0) == jnp.broadcast_to(expert[0:1], (128, ROWS))
        ).astype(F32).astype(BF)
        below = (
            lax.broadcasted_iota(jnp.int32, (TOK, TOK), 0) > lax.broadcasted_iota(jnp.int32, (TOK, TOK), 1)
        ).astype(F32).astype(BF)
        for s in range(8):
            part = slice(s * TOK, (s + 1) * TOK)
            named = (tokaux[a, part, :].astype(F32) != 0.0).astype(F32)
            code = (mm(below, named.astype(BF)) + 1.0) * named
            want = jnp.where(source[0:1] == s, (place[0:1] + 1).astype(F32), -1.0)
            hot = (mm(code.astype(BF), pick) == jnp.broadcast_to(want, (TOK, ROWS))).astype(F32)
            gatt[a, part, :] = hot.astype(BF)
            gat[a, :, part] = jnp.transpose(hot).astype(BF)

    def swaps():
        swap_x = (pu * 4 + sr) * MSG + (sc * 4 + pv) * 6 + place
        swap_y = (sr * 4 + pv) * MSG + (sc * 4 + pu) * 6 + place
        at = lax.broadcasted_iota(jnp.int32, (ROWS, ROWS), 0)
        for a, to in ((0, swap_x), (1, swap_y)):
            perm[a] = (at == jnp.broadcast_to(to[0:1], (ROWS, ROWS))).astype(F32).astype(BF)

    def norm():
        await_bytes(hid, i_sem.at[1])
        total = jnp.zeros((TOK, CW), F32)
        for k in range(NC):
            h = hid[:, k * CW : (k + 1) * CW].astype(F32)
            total = total + h * h
        inv = lax.rsqrt(jnp.sum(total, axis=1, keepdims=True) * (1.0 / D) + 1e-06)
        inv_s[...] = jnp.broadcast_to(inv, (TOK, 128))
        for k in range(NC):
            cols = slice(k * CW, (k + 1) * CW)
            unit = hid[:, cols].astype(F32) * inv
            tok[NC + k, own(frame((NC + k + 1) % 3)), :] = (unit * gain[:, cols]).astype(BF)

    norm()
    for a in (1, 2, 0):
        f = frame(a)
        await_once(tokaux.at[a], aux_r.at[a], 3 * TOK)
        for d in (1, 3, 2):
            at = ring_rows(f, d)
            put(tokaux.at[a, at], tokaux.at[a, at], aux_ss.at[a], aux_s.at[a], sib)
    for i in range(3):
        ag_second(i)
    build(1)
    for i in range(3):
        ag_third(i)
    for i in range(3, 6):
        ag_first(i)
    swaps()
    ag_second(3)

    def spread(f, buf, dst, rs, self_sem):
        mine = rows(f.place() * MSG, MSG)
        for p, d in f.peers():
            put(sbuf.at[buf, rows(p * MSG, MSG)], dst.at[mine], a_ss.at[buf], rs, d)
        pltpu.make_async_copy(sbuf.at[buf, mine], dst.at[mine], self_sem).start()

    def await_spread(dst, rs, self_sem):
        await_once(dst, rs, 15 * MSG)
        await_once(dst, self_sem, MSG)

    def await_sbuf(buf):
        await_once(sbuf.at[buf], a_ss.at[buf], 15 * MSG)

    def by_rows(step):
        def body(r, cc):
            step(rows(r * RB, RB, RB))
            return cc

        lax.fori_loop(0, ROWS // RB, body, 0)

    def reorder(a, src, dst):
        @pl.when(a == 2)
        def _():
            dst[...] = src[...]

        @pl.when(a != 2)
        def _():
            def step(at):
                dst[at, :] = mm(perm[jnp.minimum(a, 1), at, :], src[...]).astype(BF)

            by_rows(step)

    def dispatch(i, carry):
        @pl.when(i < 2 * NC)
        def _():
            buf = lax.rem(i, NS)
            a = axis(i)

            @pl.when(jnp.logical_and(i >= 1, i < 3))
            def _():
                build(a)

            await_once(tok.at[i], ag_sr.at[i], 4 * TOK)

            @pl.when(i >= NS)
            def _():
                await_sbuf(buf)

            def gather(at):
                sbuf[buf, at, :] = mm(gat[a, at, :], tok[i]).astype(BF)

            by_rows(gather)
            await_once(tok.at[i], ag_ss.at[i], 7 * TOK)
            spread(frame(a), buf, rcv.at[i], a_rs.at[i], a_self.at[i])

        @pl.when(i == 1)
        def _():
            saux[...] = mm(gat[2], tokaux[2]).astype(BF)
            mine = rows(zf.place() * MSG, MSG)
            for p, d in zf.peers():
                put(saux.at[rows(p * MSG, MSG)], raux.at[mine], x_ss.at[1], x_rs.at[2], d)
            pltpu.make_async_copy(saux.at[mine], raux.at[mine], x_self.at[0]).start()

        @pl.when(i >= LAG)
        def _():
            j = i - LAG
            await_spread(rcv.at[j], a_rs.at[j], a_self.at[j])

            @pl.when(j < NC)
            def _():
                reorder(axis(j), rcv.at[j], canon)
                wd_copy(j).wait()

                def step(at):
                    got = mm_nt(canon[at, :], wdb[lax.rem(j, 2)])

                    @pl.when(j == 0)
                    def _():
                        acc[2, at, :] = got

                    @pl.when(j > 0)
                    def _():
                        acc[2, at, :] += got

                by_rows(step)

                @pl.when(j + 2 < NC)
                def _():
                    wd_copy(j + 2).start()

            @pl.when(j >= NC)
            def _():
                n = j - NC
                reorder(axis(j), rcv.at[j], rcv.at[n])
                for cp in wgu_copies(n):
                    cp.wait()

                def step(at):
                    for m, w in ((0, wgb), (1, wub)):
                        got = mm(rcv[n, at, :], w[lax.rem(n, 2)])

                        @pl.when(n == 0)
                        def _():
                            acc[m, at, :] = got

                        @pl.when(n > 0)
                        def _():
                            acc[m, at, :] += got

                by_rows(step)
                for cp in wgu_copies(n + 2):
                    cp.start()

        @pl.when(i == 0)
        def _():
            for n in range(4, L2):
                ag_second(n)
            for n in range(6, L1):
                ag_first(n)

        @pl.when(i + L1 < 2 * NC)
        def _():
            ag_first(i + L1)

        @pl.when(i + L3 < 2 * NC)
        def _():
            ag_third(i + L3)

        @pl.when(i + L2 < 2 * NC)
        def _():
            ag_second(i + L2)

        return carry

    lax.fori_loop(0, 2 * NC - 1 + LAG, dispatch, 0)

    pl.semaphore_signal(free_sib, inc=1, device_id=sib, device_id_type=MESH)
    for a in range(3):
        for d in (1, 3):
            pl.semaphore_signal(free_ring, inc=1, device_id=frame(a).ring(d), device_id_type=MESH)

    await_once(raux, x_rs.at[2], 15 * MSG)
    await_once(raux, x_self.at[0], MSG)
    await_once(saux, x_ss.at[1], 15 * MSG)
    alane = lax.broadcasted_iota(jnp.int32, (AB, 128), 1)

    def activate(at):
        scale = jnp.sum(jnp.where(alane == me, raux[at, :].astype(F32), 0.0), axis=1, keepdims=True)
        comb = jnp.zeros((AB, 1), F32)
        for half in range(2):
            cols = slice(half * CW, (half + 1) * CW)
            gate, up, back = acc[0, at, cols], acc[1, at, cols], acc[2, at, cols]
            sig = jax.nn.sigmoid(gate)
            act = gate * sig
            comb = comb + jnp.sum(act * up * back, axis=1, keepdims=True)
            scaled = scale * back
            rcv[NC + half, at, :] = (scaled * up * sig * (1.0 + gate * (1.0 - sig))).astype(BF)
            rcv[NC + 2 + half, at, :] = (scaled * act).astype(BF)
        caux[at, :] = jnp.where(alane == me, comb, 0.0).astype(BF)

    def slot_rows(at, n):
        b = lax.rem(n, 2)
        got = mm_nt(rcv[NC, at, :], wgb[b, :, 0:CW])
        got = got + mm_nt(rcv[NC + 1, at, :], wgb[b, :, CW:H])
        got = got + mm_nt(rcv[NC + 2, at, :], wub[b, :, 0:CW])
        got = got + mm_nt(rcv[NC + 3, at, :], wub[b, :, CW:H])
        return got.astype(BF)

    def gain_sum(cut, k, at):
        return jnp.sum(cut.astype(F32) * rcv[k, at, :].astype(F32), axis=0, keepdims=True)

    QB = 4 * MSG
    LAST = 2 * NC - 1
    first_buf = (2 * NC) % NS
    await_spread(rcv.at[LAST], a_rs.at[LAST], a_self.at[LAST])
    for n in (NC - 1, NC):
        for cp in wgu_copies(n):
            cp.wait()
    await_sbuf(first_buf)
    z_mine = rows(zf.place() * MSG, MSG)

    def turn_round(t, gsum):
        du = lax.rem(t + 1, 4)
        u = lax.rem(zf.u + du, 4)
        at = rows(u * QB, QB)
        got = rcv[LAST, at, :]
        rcv[NC - 1, at, :] = got
        acc[0, at, :] += mm(got, wgb[(NC - 1) % 2])
        acc[1, at, :] += mm(got, wub[(NC - 1) % 2])
        for r in range(QB // AB):
            activate(rows(u * QB + r * AB, AB))
        cut = slot_rows(at, NC)
        sbuf[first_buf, at, :] = cut
        for dv in range(4):
            v = lax.rem(zf.v + dv, 4)
            src = sbuf.at[first_buf, rows((u * 4 + v) * MSG, MSG)]
            to = device(*zf.coords(u, v, zf.r), c)
            if dv:
                put(src, tok.at[0, z_mine], a_ss.at[first_buf], r_rs.at[0], to)
            else:

                @pl.when(du != 0)
                def _():
                    put(src, tok.at[0, z_mine], a_ss.at[first_buf], r_rs.at[0], to)

                @pl.when(du == 0)
                def _():
                    pltpu.make_async_copy(src, tok.at[0, z_mine], r_self.at[0]).start()

        return gsum + gain_sum(cut, 0, at)

    gstage[:, 0:CW] = lax.fori_loop(0, 4, turn_round, jnp.zeros((1, CW), F32))
    for n in (NC + 1, NC + 2):
        for cp in wgu_copies(n):
            cp.start()

    half_me, half_sib = rows(c * 512, 512, 512), rows((1 - c) * 512, 512, 512)

    def col_half(k):
        return pl.ds(pl.multiple_of(lax.rem(k, 2) * CW, CW), CW)

    def own_part(k):
        return 2 * lax.div(lax.rem(k, 4), 2)

    def grad_rows(k):
        return rows(lax.div(k, 2) * TOK, TOK, TOK)

    def send_back(i):
        n = i + NC
        a = back_axis(i)
        buf = lax.rem(i + 2 * NC, NS)
        for cp in wgu_copies(n):
            cp.wait()

        def step(r, gsum):
            at = rows(r * RB, RB, RB)
            cut = slot_rows(at, n)
            canon[at, :] = cut
            return gsum + gain_sum(cut, i, at)

        gsum = lax.fori_loop(0, ROWS // RB, step, jnp.zeros((1, CW), F32))
        gstage[:, pl.ds(pl.multiple_of(i * CW, CW), CW)] = gsum
        await_sbuf(buf)
        reorder(a, canon, sbuf.at[buf])
        spread(frame(a), buf, tok.at[i], r_rs.at[i], r_self.at[i])

        @pl.when(i + 2 < NC)
        def _():
            for cp in wgu_copies(n + 2):
                cp.start()

    def combine(k):
        b = lax.rem(k, 2)
        a = back_axis(k)
        await_spread(tok.at[k], r_rs.at[k], r_self.at[k])

        @pl.when(k >= 2)
        def _():
            await_bytes(pbuf.at[b], p_ss.at[b])

        pbuf[b] = mm(gatt[a, half_sib, :], tok[k, 0:ROWS, :]).astype(BF)
        put(pbuf.at[b], tok.at[NC + k, pl.ds(0, 512)], p_ss.at[b], p_rs.at[k], sib)
        acc[own_part(k), 0:512, col_half(k)] = mm(gatt[a, half_me, :], tok[k, 0:ROWS, :])

    def both_cores(k, f, d):
        at = rows(lax.rem(f.r + d, 4) * TOK, TOK, TOK)
        return acc[own_part(k), at, col_half(k)] + tok[NC + k, at, :].astype(F32)

    def relay(k):
        b = lax.rem(k, 2)
        f = frame(back_axis(k))
        await_bytes(tok.at[NC + k, pl.ds(0, 512)], p_rs.at[k])

        @pl.when(k >= 2)
        def _():
            await_bytes(q1buf.at[b], q1_ss.at[b])

        q1buf[b] = both_cores(k, f, 2).astype(BF)
        for d, part in ((1, 0), (3, HALF)):
            put(
                q1buf.at[b, pl.ds(part, HALF)], tok.at[NC + k, pl.ds(512 + part, HALF)],
                q1_ss.at[b], q1_rs.at[k], f.ring(d),
            )

    def scatter(k):
        b = lax.rem(k, 2)
        f = frame(back_axis(k))
        await_bytes(tok.at[NC + k, pl.ds(512, TOK)], q1_rs.at[k])

        @pl.when(k >= 2)
        def _():
            await_bytes(q2buf.at[b], q2_ss.at[b])

        on = both_cores(k, f, 1)
        q2buf[b, 0:HALF, :] = (on[0:HALF] + tok[NC + k, 512 : 512 + HALF, :].astype(F32)).astype(BF)
        q2buf[b, HALF:TOK, :] = on[HALF:TOK].astype(BF)
        on = both_cores(k, f, 3)
        q2buf[b, TOK : TOK + HALF, :] = on[0:HALF].astype(BF)
        q2buf[b, TOK + HALF : 2 * TOK, :] = (
            on[HALF:TOK] + tok[NC + k, 512 + HALF : 512 + TOK, :].astype(F32)
        ).astype(BF)
        for d, part in ((1, 0), (3, TOK)):
            put(
                q2buf.at[b, pl.ds(part, TOK)], tok.at[NC + k, pl.ds(640 + part, TOK)],
                q2_ss.at[b], q2_rs.at[k], f.ring(d),
            )
        acc[1, grad_rows(k), col_half(k)] = both_cores(k, f, 0)

    def settle(k):
        await_bytes(tok.at[NC + k, pl.ds(640, 2 * TOK)], q2_rs.at[k])
        grad = acc[1, grad_rows(k), col_half(k)]
        for d in range(2):
            grad = grad + tok[NC + k, 640 + d * TOK : 640 + (d + 1) * TOK, :].astype(F32)
        cols = pl.ds(pl.multiple_of(k * CW, CW), CW)
        scaled = grad * gain[:, cols]
        acc[1, grad_rows(k), col_half(k)] = scaled
        proj_s[...] += scaled * (hid[:, cols].astype(F32) * inv_s[:, 0:1])

    proj_s[...] = jnp.zeros_like(proj_s)

    def back(i, carry):
        @pl.when(i == K1)
        def _():
            pl.semaphore_wait(free_sib, 1)
            pl.semaphore_wait(free_ring, 6)

        @pl.when(jnp.logical_and(i >= 1, i < NC))
        def _():
            send_back(i)

        @pl.when(jnp.logical_and(i >= K3, i < NC + K3))
        def _():
            scatter(i - K3)

        @pl.when(jnp.logical_and(i >= K2, i < NC + K2))
        def _():
            relay(i - K2)

        @pl.when(jnp.logical_and(i >= K1, i < NC + K1))
        def _():
            combine(i - K1)

        @pl.when(i == 0)
        def _():
            mine = rows(zf.place() * MSG, MSG)
            for p, d in zf.peers():
                put(caux.at[rows(p * MSG, MSG)], cret.at[mine], x_ss.at[2], x_rs.at[3], d)
            pltpu.make_async_copy(caux.at[mine], cret.at[mine], x_self.at[1]).start()

        @pl.when(i == 3)
        def _():
            await_once(cret, x_rs.at[3], 15 * MSG)
            await_once(cret, x_self.at[1], MSG)
            await_once(caux, x_ss.at[2], 15 * MSG)
            paux[...] = mm(gatt[2, half_sib, :], cret[...]).astype(BF)
            put(paux, sibaux, x_ss.at[3], x_rs.at[4], sib)

        @pl.when(i == 5)
        def _():
            await_bytes(sibaux, x_rs.at[4])
            await_bytes(paux, x_ss.at[3])
            qaux[...] = (mm(gatt[2, half_me, :], cret[...]) + sibaux[...].astype(F32)).astype(BF)
            for d in (1, 2, 3):
                at = rows(((z + d) % 4) * TOK, TOK, TOK)
                put(qaux.at[at], ringaux.at[pl.ds((d - 1) * TOK, TOK)], x_ss.at[4], x_rs.at[5], zf.ring(d))

        @pl.when(i == NC - 1)
        def _():
            gall[zf.place()] = gstage[...]
            for _, d in zf.peers():
                put(gall.at[zf.place()], gall.at[zf.place()], g_ss.at[0], g_rs.at[0], d)

        @pl.when(i == NC)
        def _():
            await_once(gall, g_rs.at[0], 15)
            await_once(gall, g_ss.at[0], 15)
            gring[z] = jnp.sum(gall[...], axis=0)
            for d in (1, 2, 3):
                put(gring.at[z], gring.at[z], g_ss.at[1], g_rs.at[1], zf.ring(d))

        @pl.when(i == NC + 1)
        def _():
            await_once(gring, g_rs.at[1], 3)
            await_once(gring, g_ss.at[1], 3)
            gsib[c] = gring[0] + gring[1] + gring[2] + gring[3]
            put(gsib.at[c], gsib.at[c], g_ss.at[2], g_rs.at[2], sib)

        @pl.when(i >= K4)
        def _():
            settle(i - K4)

        return carry

    lax.fori_loop(0, NC + K4, back, 0)

    project = jnp.sum(proj_s[...], axis=1, keepdims=True) * (1.0 / D)
    inv = inv_s[:, 0:1]
    for k in range(NC):
        cols = slice(k * CW, (k + 1) * CW)
        scaled = acc[1, (k // 2) * TOK : (k // 2 + 1) * TOK, (k % 2) * CW : (k % 2 + 1) * CW]
        unit = hid[:, cols].astype(F32) * inv
        out_ref[:, cols] = (inv * (scaled - unit * project)).astype(BF)

    await_once(gsib, g_rs.at[2], 1)
    await_once(gsib, g_ss.at[2], 1)
    for r in range(D // 128):
        cols = slice(r * 128, (r + 1) * 128)
        gout_ref[r : r + 1, :] = (gsib[0, :, cols] + gsib[1, :, cols]) / gain[:, cols]

    await_bytes(ringaux, x_rs.at[5])
    await_bytes(ringaux, x_ss.at[4])
    cfin = qaux[rows(z * TOK, TOK, TOK), :].astype(F32)
    for d in range(3):
        cfin = cfin + ringaux[d * TOK : (d + 1) * TOK, :].astype(F32)
    picked = jnp.zeros((TOK, 128), F32)
    named_by = jnp.transpose(turn[...])
    for k in range(4):
        got = jnp.sum(jnp.where(named_by[:, k : k + 1] == lane_f, cfin, 0.0), axis=1, keepdims=True)
        picked = jnp.where(lane == k, got, picked)
    cout_ref[...] = jnp.transpose(picked)[0:4, :].astype(BF)

    for b in range(NS):
        await_sbuf(b)
    for b in range(2):
        await_bytes(pbuf.at[b], p_ss.at[b])
        await_bytes(q1buf.at[b], q1_ss.at[b])
        await_bytes(q2buf.at[b], q2_ss.at[b])


def hand_over(*refs):
    for src, dst in zip(refs[0:3], refs[3:6]):
        dst[...] = src[...]


def shards(hidden_in, norm_gain, upstream, routes, combine_fixed, w_gate, w_up, w_down):
    vm = pl.BlockSpec(memory_space=pltpu.VMEM)
    hbm = pl.BlockSpec(memory_space=pl.ANY)
    dma = pltpu.SemaphoreType.DMA
    shapes = (
        jax.ShapeDtypeStruct((TOK, D), BF),
        jax.ShapeDtypeStruct((D // 128, 128), F32),
        jax.ShapeDtypeStruct((4, TOK), BF),
    )
    results = pl.pallas_call(
        kernel,
        out_shape=shapes,
        in_specs=[hbm, vm, hbm, vm, vm, hbm, hbm, hbm],
        out_specs=(vm, vm, vm),
        scratch_shapes=[
            pltpu.VMEM((2 * NC, GTOK, CW), BF),
            pltpu.VMEM((3, GTOK, 128), BF),
            pltpu.VMEM((3, ROWS, GTOK), BF),
            pltpu.VMEM((3, GTOK, ROWS), BF),
            pltpu.VMEM((2, ROWS, ROWS), BF),
            pltpu.VMEM((NS, ROWS, CW), BF),
            pltpu.VMEM((ROWS, 128), BF),
            pltpu.VMEM((2 * NC, ROWS, CW), BF),
            pltpu.VMEM((ROWS, 128), BF),
            pltpu.VMEM((ROWS, CW), BF),
            pltpu.VMEM((3, ROWS, H), F32),
            pltpu.VMEM((TOK, D), BF),
            pltpu.VMEM((1, D), F32),
            pltpu.VMEM((8, TOK), F32),
            pltpu.VMEM((2, H, CW), BF),
            pltpu.VMEM((2, CW, H), BF),
            pltpu.VMEM((2, CW, H), BF),
            pltpu.VMEM((ROWS, 128), BF),
            pltpu.VMEM((ROWS, 128), BF),
            pltpu.VMEM((2, 512, CW), BF),
            pltpu.VMEM((512, 128), BF),
            pltpu.VMEM((2, TOK, CW), BF),
            pltpu.VMEM((2, 2 * TOK, CW), BF),
            pltpu.VMEM((512, 128), BF),
            pltpu.VMEM((512, 128), BF),
            pltpu.VMEM((384, 128), BF),
            pltpu.VMEM((TOK, 128), F32),
            pltpu.VMEM((TOK, CW), F32),
            pltpu.VMEM((16, 1, D), F32),
            pltpu.VMEM((4, 1, D), F32),
            pltpu.VMEM((2, 1, D), F32),
            pltpu.VMEM((1, D), F32),
            dma((2,)),
            dma((3, 2)),
            dma((2 * NC,)),
            dma((2 * NC,)),
            dma((2 * NC,)),
            dma((2 * NC,)),
            dma((3,)),
            dma((3,)),
            dma((3,)),
            dma((NS,)),
            dma((2 * NC,)),
            dma((2 * NC,)),
            dma((5,)),
            dma((6,)),
            dma((2,)),
            dma((NC,)),
            dma((NC,)),
            dma((2,)),
            dma((NC,)),
            dma((2,)),
            dma((NC,)),
            dma((2,)),
            dma((NC,)),
            dma((3,)),
            dma((3,)),
            pltpu.SemaphoreType.REGULAR,
            pltpu.SemaphoreType.REGULAR,
        ],
        compiler_params=pltpu.CompilerParams(
            collective_id=0, has_side_effects=True, vmem_limit_bytes=63 * 2**20
        ),
        cost_estimate=pl.CostEstimate(flops=50 * 10**9, bytes_accessed=40 * 10**6, transcendentals=10**6),
    )(hidden_in, norm_gain.reshape(D // 128, 128), upstream, routes.T, combine_fixed.T, w_gate, w_up, w_down)
    out, gain_grad, combine_grad = pl.pallas_call(
        hand_over,
        out_shape=shapes,
        in_specs=[vm] * 3,
        out_specs=(vm,) * 3,
    )(*results)
    return out, gain_grad.reshape(D), combine_grad.T


def solution(mesh):
    split = ("expert", "tensor")
    in_specs = (
        P(split, None),
        P(),
        P(split, None),
        P(split, None),
        P(split, None),
        P(split, None, None),
        P(split, None, None),
        P(split, None, None),
    )
    out_specs = (P(split, None), P(), P(split, None))
    return jax.shard_map(shards, mesh=mesh, in_specs=in_specs, out_specs=out_specs, check_vma=False)
```
